512 devices in a mesh: ops: 128 (over z, x_hi, y), sec: 4 (over x_lo, core).
Axes of the slice: x: 4 (x_hi: 2, x_lo: 2; x = x_hi * 2 + x_lo), y: 4, z: 16, core: 2. Of those that a mesh axis runs over, the one named last changes fastest.
Arguments:
- wave: bfloat16 [4, 256, 256], P('sec', 'ops'), may hold values from -12 to 12
- sector_live: int32 [4], P('sec'), may hold values from 128 to 256, as said below
- left_ops: bfloat16 [4, 1536, 256, 256], P('sec', 'ops'), may hold values from -24 to 24
- right_ops: bfloat16 [4, 1536, 256, 256], P('sec', 'ops'), may hold values from -0.375 to 0.375
- pair_shift: int32 [1536], P('ops'), may hold values from -2 to 2
- pair_orbitals: int32 [1536, 2], P('ops'), may hold values from 0 to 119
- orbital_scale: float32 [120], replicated, may hold values from 0.5 to 2
- block_ham: bfloat16 [4, 256, 256], P('sec', 'ops'), may hold values from -1 to 4
- site_basis: bfloat16 [4, 256, 256], P('sec', 'ops'), may hold values from -0.375 to 0.375
Outputs:
- residual: float32 [4, 256, 256], P('sec', 'ops')
- renormalized: bfloat16 [4, 1536, 256, 256], P('sec', 'ops')
The draws below stay inside these ranges and needn't reach their ends.
Inputs may be any that keep to these rules, and one draw needn't show every extreme that they name: `sector_live`: in every draw some sector has all 256 rows live.
All inputs are finite; a program needn't handle non-finite values.
Results may differ from the reference program's by a relative error of at most 0.0049.
Values may be sent and summed in bfloat16 or wider, within the bound.
A program may use at most 64 MiB of HBM per device.

```python
import math
import jax
import jax.numpy as jnp
from jax import lax

NORB = 120
SD = 256
SDN = 256
NSEC = 4
NPAIR = 1536


def draw_wave(key, part):
    key = jax.random.fold_in(key, 1)
    first_key = jax.random.fold_in(key, 0)
    row_pos = jnp.arange(SD, dtype=jnp.float32) / (SD - 1)
    rising = jnp.exp(math.log(3.0) * row_pos)[None, :, None]
    values = jnp.clip(jax.random.normal(first_key, (NSEC, SD, SD), jnp.float32), -4.0, 4.0)
    return (values * rising).astype(jnp.bfloat16)


def draw_sector_live(key, part):
    key = jax.random.fold_in(key, 2)
    first_key, second_key = jax.random.split(key)
    sizes = jax.random.randint(first_key, (NSEC,), SD // 2, SD + 1)
    chosen = jax.random.randint(second_key, (), 0, NSEC)
    return jnp.where(jnp.arange(NSEC, dtype=jnp.int32) == chosen, SD, sizes).astype(jnp.int32)


def draw_block_ham(key, part):
    key = jax.random.fold_in(key, 3)
    first_key, second_key = jax.random.split(key)
    spread = jnp.clip(jax.random.normal(first_key, (NSEC, SD, SD), jnp.float32), -4.0, 4.0)
    spread = spread / math.sqrt(SD)
    level = jnp.exp(jax.random.uniform(second_key, (NSEC, SD, 1), jnp.float32, 0.0, math.log(3.0)))
    diagonal = (jnp.arange(SD)[:, None] == jnp.arange(SD)[None, :])[None, :, :]
    return (spread + jnp.where(diagonal, level, 0.0)).astype(jnp.bfloat16)


def place_ends(drawn, key, smallest, largest):
    longest = drawn.shape.index(max(drawn.shape))
    spots = []
    for shift in (0, 1):
        where = [jax.random.randint(jax.random.fold_in(key, axis), (), 0, length) for axis, length in enumerate(drawn.shape)]
        where[longest] = (where[longest] + shift) % drawn.shape[longest]
        spots.append(tuple(where))
    return drawn.at[spots[0]].set(smallest).at[spots[1]].set(largest)


def spiked(result, own_key, source, target, parts, factor):
    owner, partner = [(jnp.arange(result.shape[position]) // (result.shape[position] // parts)).reshape([-1 if axis == position else 1 for axis in range(result.ndim)]) for position in (source, target)]
    chosen = jax.random.permutation(own_key, parts)[partner]
    strong = (owner == chosen) | (owner == (partner + parts // 2) % parts)
    return jnp.where(strong, factor * result, result)


def levels(key, dims, shards, least, largest):
    def one(dim, blocks):
        draws = jax.random.uniform(jax.random.fold_in(jax.random.fold_in(key, 6), dim), (blocks,), jnp.float32, least / len(shards), largest / len(shards))
        return jnp.repeat(jnp.exp(draws), dims[dim] // blocks).reshape((-1,) + (1,) * (len(dims) - dim - 1))

    loudness = one(*shards[0])
    for cut in shards[1:]:
        loudness = loudness * one(*cut)
    return loudness


def gaussian(rng, extent, scale, bound, shards=(), kind=jnp.bfloat16):
    loudness = levels(rng, extent, shards, -0.22, 0.18) if shards else 1.0
    entries = jax.random.normal(rng, extent, jnp.float32) * scale * loudness
    return jnp.minimum(jnp.maximum(entries, -bound), bound).astype(kind)


def gaussian_with(stream_key, dims, deviation, reach, shards, heavy, kind=jnp.bfloat16):
    entries = deviation * jax.random.normal(stream_key, dims, jnp.float32)
    if shards:
        entries = entries * levels(stream_key, dims, shards, -0.22, 0.18)
    return jnp.clip(spiked(entries, jax.random.fold_in(stream_key, 3), *heavy), -reach, reach).astype(kind)


def setup_inputs(seed: int = 0) -> dict:
    arg_keys = jax.random.split(jax.random.key(seed), 10)
    wave = draw_wave(jax.random.fold_in(arg_keys[9], 71), 0)
    sector_live = draw_sector_live(jax.random.fold_in(arg_keys[9], 71), 0)
    left_ops = gaussian_with(arg_keys[2], (NSEC, NPAIR, SD, SD), 1.0, 24.0, ((0, 4), (1, 128)), (1, 2, 128, 5.5))
    right_ops = gaussian(arg_keys[3], (NSEC, NPAIR, SD, SD), SD ** -0.5, 0.375, ((0, 4), (1, 128)))
    pair_shift = place_ends(jax.random.randint(arg_keys[4], (NPAIR,), 0 - NSEC // 2, NSEC // 2 + 1), jax.random.fold_in(arg_keys[4], 1), 0 - NSEC // 2, (NSEC // 2 + 1) - 1).astype(jnp.int32)
    pair_orbitals = place_ends(jax.random.randint(arg_keys[5], (NPAIR, 2), 0, NORB), jax.random.fold_in(arg_keys[5], 1), 0, NORB - 1).astype(jnp.int32)
    orbital_scale = jnp.clip(jnp.exp(jax.random.uniform(arg_keys[6], (NORB,), jnp.float32, math.log(0.5), math.log(2.0))), 0.5, 2.0)
    block_ham = draw_block_ham(jax.random.fold_in(arg_keys[9], 71), 0)
    site_basis = gaussian(arg_keys[8], (NSEC, SD, SDN), SD ** -0.5, 0.375, ((0, 4), (1, 128)))
    return dict(wave=wave, sector_live=sector_live, left_ops=left_ops, right_ops=right_ops, pair_shift=pair_shift, pair_orbitals=pair_orbitals, orbital_scale=orbital_scale, block_ham=block_ham, site_basis=site_basis)


def reference(wave, sector_live, left_ops, right_ops, pair_shift, pair_orbitals, orbital_scale, block_ham, site_basis):
    row_ids = jnp.arange(SD, dtype=jnp.int32)
    keep_mask = row_ids[None, :] < sector_live[:, None]
    masked = jnp.where(keep_mask[:, :, None] & keep_mask[:, None, :], wave, jnp.zeros_like(wave))
    one_hot = (pair_orbitals[:, :, None] == jnp.arange(NORB, dtype=jnp.int32)[None, None, :]).astype(jnp.float32)
    scales = lax.optimization_barrier(jnp.sum(one_hot * orbital_scale[None, None, :], axis=2))
    coupling = scales[:, 0] * scales[:, 1] / math.sqrt(SD * NPAIR)
    sigma_list = []
    renorm_list = []
    for sector in range(NSEC):
        source = (sector - pair_shift).astype(jnp.int32)
        in_range = (source >= 0) & (source < NSEC)
        clipped = jnp.clip(source, 0, NSEC - 1).astype(jnp.int32)
        weight_used = jnp.where(in_range, coupling, jnp.zeros_like(coupling))
        target_basis = site_basis[sector]

        def add_pair(total, pieces):
            left_op, right_op, src, inside, factor = pieces
            wave_src = lax.dynamic_index_in_dim(masked, src, 0, keepdims=False)
            basis_src = lax.dynamic_index_in_dim(site_basis, src, 0, keepdims=False)
            carried = (factor * jnp.dot(wave_src, right_op.T, preferred_element_type=jnp.float32)).astype(jnp.bfloat16)
            total = total + jnp.dot(left_op, carried, preferred_element_type=jnp.float32)
            left_basis = jnp.dot(left_op, basis_src, preferred_element_type=jnp.float32).astype(jnp.bfloat16)
            renormed = jnp.dot(target_basis.T, left_basis, preferred_element_type=jnp.float32)
            renormed = jnp.where(inside, renormed, jnp.zeros_like(renormed)).astype(jnp.bfloat16)
            return (total, renormed)
        summed, renormed = lax.scan(add_pair, jnp.zeros((SD, SD), jnp.float32), (left_ops[sector], right_ops[sector], clipped, in_range, weight_used))
        summed = summed + jnp.dot(block_ham[sector], masked[sector], preferred_element_type=jnp.float32)
        sigma_list.append(summed)
        renorm_list.append(renormed)
    sigma = jnp.stack(sigma_list)
    masked_wide = masked.astype(jnp.float32)
    energy = jnp.sum(masked_wide * sigma) / jnp.sum(masked_wide * masked_wide)
    residual = sigma - energy * masked_wide
    return (residual, jnp.stack(renorm_list))
```

```python
import functools
import math

import jax
import jax.numpy as jnp
from jax import lax
from jax.experimental import pallas as pl
from jax.experimental.pallas import tpu as pltpu
from jax.sharding import PartitionSpec as P

MESH = pl.DeviceIdType.MESH
F32 = jnp.float32
BF16 = jnp.bfloat16
NZ = 16
NJ = 8
NX = 16
NSEC = 4
NPAIR = 12
D = 256
H = 128
SCALE = 1.0 / math.sqrt(256 * 1536)


def nt(a, b):
    return lax.dot_general(a, b, (((1,), (1,)), ((), ())), preferred_element_type=F32)


def nn(a, b):
    return jnp.dot(a, b, preferred_element_type=F32)


def kernel(
    live_ref,
    shift_ref,
    orb_ref,
    scale_ref,
    wave_ref,
    ham_ref,
    basis_ref,
    left_hbm,
    right_hbm,
    resid_ref,
    renorm_hbm,
    left,
    right,
    carried,
    renorm,
    zbuf,
    wall,
    mats,
    perm,
    basis_t,
    sig,
    rs_send,
    rs_recv,
    corr_own,
    corr_sib,
    corr_x,
    zs_send,
    zs_recv,
    load_sem,
    out_sem,
    zsend_sem,
    zrecv_sem,
    xsend_sem,
    xrecv_sem,
    csend_sem,
    crecv_sem,
    rsend_sem,
    rrecv_sem,
    ksend_sem,
    krecv_sem,
    qsend_sem,
    qrecv_sem,
    ssend_sem,
    srecv_sem,
):
    ops = lax.axis_index("ops")
    sec = lax.axis_index("sec")
    z = ops // NJ
    j = ops % NJ
    x_lo = sec // 2
    core = sec % 2
    plane = x_lo * NJ + j

    def at_z(i):
        return {"ops": lax.rem(z + i, NZ) * NJ + j, "sec": sec}

    def at_plane(i):
        p = lax.rem(plane + i, NX)
        return {"ops": z * NJ + p % NJ, "sec": (p // NJ) * 2 + core}

    sibling = {"ops": ops, "sec": x_lo * 2 + (1 - core)}

    def remote(src, dst, send, recv, device):
        return pltpu.make_async_remote_copy(
            src_ref=src, dst_ref=dst, send_sem=send, recv_sem=recv, device_id=device, device_id_type=MESH
        )

    def taken(ref, sem):
        pltpu.make_async_copy(ref, ref, sem).wait()

    for k in range(NPAIR):
        pltpu.make_async_copy(right_hbm.at[0, k], right.at[k], load_sem.at[0]).start()
    for k in range(NPAIR):
        pltpu.make_async_copy(left_hbm.at[0, k], left.at[k], load_sem.at[1]).start()

    barrier = pltpu.get_barrier_semaphore()

    def greet_z(i, _):
        pl.semaphore_signal(barrier, inc=1, device_id=at_z(i), device_id_type=MESH)
        return 0

    def greet_plane(i, _):
        pl.semaphore_signal(barrier, inc=1, device_id=at_plane(i), device_id_type=MESH)
        return 0

    lax.fori_loop(1, NZ, greet_z, 0)
    lax.fori_loop(1, NX, greet_plane, 0)
    pl.semaphore_signal(barrier, inc=1, device_id=sibling, device_id_type=MESH)

    live = live_ref[0]
    row_ids = ops * 2 + lax.broadcasted_iota(jnp.int32, (2, D), 0)
    col_ids = lax.broadcasted_iota(jnp.int32, (2, D), 1)
    keep = (row_ids < live) & (col_ids < live)
    masked_rows = jnp.where(keep, wave_ref[0].astype(F32), 0.0)
    basis_rows = basis_ref[0].astype(F32)
    for h in range(2):
        zbuf[0, z, 2 * h : 2 * h + 2, :] = masked_rows[:, h * H : (h + 1) * H]
        zbuf[1, z, 2 * h : 2 * h + 2, :] = basis_rows[:, h * H : (h + 1) * H]

    m_ids = lax.broadcasted_iota(jnp.int32, (D, D), 0)
    s_ids = lax.broadcasted_iota(jnp.int32, (D, D), 1)
    wanted = ((m_ids % 16) // 2) * 32 + (m_ids % 2) * 16 + m_ids // 16
    perm[0] = jnp.where(wanted == s_ids, 1.0, 0.0).astype(BF16)
    perm[1] = jnp.where(m_ids == s_ids, 1.0, 0.0).astype(BF16)

    pl.semaphore_wait(barrier, (NZ - 1) + (NX - 1) + 1)

    for w in range(2):

        def send_z(i, _):
            remote(
                zbuf.at[w, z], zbuf.at[w, z], zsend_sem.at[w], zrecv_sem.at[w], at_z(i)
            ).start()
            return 0

        lax.fori_loop(1, NZ, send_z, 0)

    slot = sec * NJ + j
    for w in range(2):
        taken(zbuf.at[w, pl.ds(0, NZ - 1)], zrecv_sem.at[w])
        for h in range(2):
            for r in range(2):
                wall[w, slot, r * 16 : (r + 1) * 16, h * H : (h + 1) * H] = zbuf[w, :, 2 * h + r, :].astype(BF16)

        def send_plane(i, _):
            remote(
                wall.at[w, slot],
                wall.at[w, slot],
                xsend_sem.at[w],
                xrecv_sem.at[w, plane],
                at_plane(i),
            ).start()
            return 0

        lax.fori_loop(1, NX, send_plane, 0)
        remote(wall.at[w, slot], wall.at[w, slot], csend_sem.at[w], crecv_sem.at[w], sibling).start()

    def pass_on(w):
        def one(i, _):
            p = lax.rem(plane + NX - i, NX)
            s = ((p // NJ) * 2 + core) * NJ + p % NJ
            taken(wall.at[w, s], xrecv_sem.at[w, p])
            remote(wall.at[w, s], wall.at[w, s], csend_sem.at[w], crecv_sem.at[w], sibling).start()
            return 0

        lax.fori_loop(1, NX, one, 0)

    def assemble(w):
        taken(wall.at[w, pl.ds(0, NX)], crecv_sem.at[w])
        for u in range(NSEC):
            stacked = wall[w, u * NJ : (u + 1) * NJ].reshape(D, D)
            mats[w, u] = nn(perm[0], stacked).astype(BF16)

    pass_on(0)
    assemble(0)

    taken(right, load_sem.at[0])

    def source(k):
        u = sec - shift_ref[k]
        inside = (u >= 0) & (u < NSEC)
        return jnp.clip(u, 0, NSEC - 1), inside

    for k in range(NPAIR):
        u, inside = source(k)
        weight = scale_ref[orb_ref[k, 0]] * scale_ref[orb_ref[k, 1]] * SCALE
        weight = jnp.where(inside, weight, 0.0)
        carried[k] = (weight * nt(mats[0, u], right[k])).astype(BF16)

    pass_on(1)

    taken(left, load_sem.at[1])
    total = nn(left[0], carried[0])
    for k in range(1, NPAIR):
        total += nn(left[k], carried[k])
    for h in range(2):
        sig[h] = total[:, h * H : (h + 1) * H]

    for t in range(NJ):
        for h in range(2):
            for r in range(2):
                rs_send[t, 2 * h + r] = sig[h, pl.ds(2 * t + r, 16, stride=16), :].astype(rs_send.dtype)

    def send_rs(i, _):
        t = lax.rem(j + i, NJ)
        remote(
            rs_send.at[t], rs_recv.at[j], rsend_sem, rrecv_sem, {"ops": z * NJ + t, "sec": sec}
        ).start()
        return 0

    lax.fori_loop(1, NJ, send_rs, 0)
    rs_recv[j] = rs_send[j]

    own_wave = mats[0, sec]
    ham_rows = nn(ham_ref[0], own_wave)
    num = jnp.sum(ham_rows * masked_rows, axis=0, keepdims=True)
    for h in range(2):
        num_h = jnp.sum(sig[h] * own_wave[:, h * H : (h + 1) * H].astype(F32), axis=0, keepdims=True)
        part = num_h + num[:, h * H : (h + 1) * H]
        lanes = part if h == 0 else lanes + part
    corr_own[...] = lanes
    remote(corr_own, corr_sib, ksend_sem, krecv_sem, sibling).start()

    assemble(1)
    basis_t[...] = nt(perm[1], mats[1, sec]).astype(BF16)

    taken(corr_sib, krecv_sem)
    corr_x[plane] = corr_own[...] + corr_sib[...]

    def send_corr(i, _):
        remote(corr_x.at[plane], corr_x.at[plane], qsend_sem, qrecv_sem, at_plane(i)).start()
        return 0

    lax.fori_loop(1, NX, send_corr, 0)

    def renormalize(ks):
        for k in ks:
            u, inside = source(k)
            left_basis = nn(left[k], mats[1, u]).astype(BF16)
            value = nn(basis_t[...], left_basis)
            renorm[k] = jnp.where(inside, value, 0.0).astype(BF16)
            pltpu.make_async_copy(renorm.at[k], renorm_hbm.at[0, k], out_sem).start()

    renormalize(range(NPAIR // 2))

    taken(rs_recv.at[pl.ds(0, NJ - 1)], rrecv_sem)
    chunk = [rs_recv[0, q].astype(F32) for q in range(4)]
    for t in range(1, NJ):
        for q in range(4):
            chunk[q] += rs_recv[t, q].astype(F32)
    for q in range(4):
        zs_send[:, q, :] = chunk[q]
    taken(corr_x.at[pl.ds(0, NX - 1)], qrecv_sem)
    zs_send[:, 4:8, :] = jnp.broadcast_to(jnp.sum(corr_x[...], axis=0, keepdims=True), (NZ, 4, H))

    def send_sum(i, _):
        t = lax.rem(z + i, NZ)
        remote(zs_send.at[t], zs_recv.at[z], ssend_sem, srecv_sem, at_z(i)).start()
        return 0

    lax.fori_loop(1, NZ, send_sum, 0)
    zs_recv[z] = zs_send[z]

    renormalize(range(NPAIR // 2, NPAIR))

    norm = jnp.zeros((D, D), F32)
    for u in range(NSEC):
        wide = mats[0, u].astype(F32)
        norm += wide * wide
    norm = jnp.sum(jnp.sum(norm, axis=0, keepdims=True), axis=1, keepdims=True)

    taken(zs_recv.at[pl.ds(0, NZ - 1)], srecv_sem)
    summed = jnp.sum(zs_recv[...], axis=0)
    energy = jnp.sum(summed[4:5, :], axis=1, keepdims=True) / norm
    for h in range(2):
        rows = summed[2 * h : 2 * h + 2, :] + ham_rows[:, h * H : (h + 1) * H]
        resid_ref[0, :, h * H : (h + 1) * H] = rows - energy * masked_rows[:, h * H : (h + 1) * H]

    for w in range(2):
        taken(zbuf.at[w, pl.ds(0, NZ - 1)], zsend_sem.at[w])
        taken(wall.at[w, pl.ds(0, NX - 1)], xsend_sem.at[w])
        taken(wall.at[w, pl.ds(0, NX)], csend_sem.at[w])
    taken(rs_send.at[pl.ds(0, NJ - 1)], rsend_sem)
    taken(corr_own, ksend_sem)
    taken(corr_x.at[pl.ds(0, NX - 1)], qsend_sem)
    taken(zs_send.at[pl.ds(0, NZ - 1)], ssend_sem)
    pltpu.make_async_copy(renorm, renorm_hbm.at[0], out_sem).wait()


RS_TYPE = BF16


def on_device(
    wave,
    sector_live,
    left_ops,
    right_ops,
    pair_shift,
    pair_orbitals,
    orbital_scale,
    block_ham,
    site_basis,
):
    smem = pl.BlockSpec(memory_space=pltpu.SMEM)
    vmem = pl.BlockSpec(memory_space=pltpu.VMEM)
    hbm = pl.BlockSpec(memory_space=pl.ANY)
    dma = pltpu.SemaphoreType.DMA
    return pl.pallas_call(
        kernel,
        out_shape=(
            jax.ShapeDtypeStruct((1, 2, D), F32),
            jax.ShapeDtypeStruct((1, NPAIR, D, D), BF16),
        ),
        in_specs=[smem] * 4 + [vmem] * 3 + [hbm] * 2,
        out_specs=(vmem, hbm),
        scratch_shapes=[
            pltpu.VMEM((NPAIR, D, D), BF16),
            pltpu.VMEM((NPAIR, D, D), BF16),
            pltpu.VMEM((NPAIR, D, D), BF16),
            pltpu.VMEM((NPAIR, D, D), BF16),
            pltpu.VMEM((2, NZ, 4, H), F32),
            pltpu.VMEM((2, NSEC * NJ, 32, D), BF16),
            pltpu.VMEM((2, NSEC, D, D), BF16),
            pltpu.VMEM((2, D, D), BF16),
            pltpu.VMEM((D, D), BF16),
            pltpu.VMEM((2, D, H), F32),
            pltpu.VMEM((NJ, 4, NZ, H), RS_TYPE),
            pltpu.VMEM((NJ, 4, NZ, H), RS_TYPE),
            pltpu.VMEM((1, H), F32),
            pltpu.VMEM((1, H), F32),
            pltpu.VMEM((NX, 1, H), F32),
            pltpu.VMEM((NZ, 8, H), F32),
            pltpu.VMEM((NZ, 8, H), F32),
            dma((2,)),
            dma,
            dma((2,)),
            dma((2,)),
            dma((2,)),
            dma((2, NX)),
            dma((2,)),
            dma((2,)),
            dma,
            dma,
            dma,
            dma,
            dma,
            dma,
            dma,
            dma,
        ],
        compiler_params=pltpu.CompilerParams(
            collective_id=0, has_side_effects=True, vmem_limit_bytes=48 * 1024 * 1024
        ),
        cost_estimate=pl.CostEstimate(flops=1900000000, bytes_accessed=4800000, transcendentals=0),
    )(
        sector_live,
        pair_shift,
        pair_orbitals,
        orbital_scale,
        wave,
        block_ham,
        site_basis,
        left_ops,
        right_ops,
    )


def solution(mesh):
    placed = (
        P("sec", "ops", None),
        P("sec"),
        P("sec", "ops", None, None),
        P("sec", "ops", None, None),
        P("ops"),
        P("ops", None),
        P(),
        P("sec", "ops", None),
        P("sec", "ops", None),
    )
    return jax.shard_map(
        on_device,
        mesh=mesh,
        in_specs=placed,
        out_specs=(P("sec", "ops", None), P("sec", "ops", None, None)),
        check_vma=False,
    )
```

```python
import functools
import math

import jax
import jax.numpy as jnp
from jax import lax
from jax.experimental import pallas as pl
from jax.experimental.pallas import tpu as pltpu
from jax.sharding import PartitionSpec as P

MESH = pl.DeviceIdType.MESH
F32 = jnp.float32
BF16 = jnp.bfloat16
NZ = 16
NJ = 8
NX = 16
NSEC = 4
NPAIR = 12
NORB = 120
D = 256
H = 128
SCALE = 1.0 / math.sqrt(256 * 1536)

Z_STEPS = sorted(range(1, NZ), key=lambda i: -min(i, NZ - i))
XY_STEPS = sorted(
    [(a, b) for a in range(4) for b in range(4) if a or b],
    key=lambda s: -(min(s[0], 4 - s[0]) + min(s[1], 4 - s[1])),
)
J_STEPS = sorted(
    [(a, b) for a in range(2) for b in range(4) if a or b],
    key=lambda s: -(2 * s[0] + min(s[1], 4 - s[1])),
)


def nt(a, b):
    return lax.dot_general(a, b, (((1,), (1,)), ((), ())), preferred_element_type=F32)


def nn(a, b):
    return jnp.dot(a, b, preferred_element_type=F32)


def kernel(
    live_hbm,
    shift_hbm,
    orb_hbm,
    scale_hbm,
    wave_hbm,
    ham_hbm,
    basis_hbm,
    left_hbm,
    right_hbm,
    resid_ref,
    renorm_ref,
    live_ref,
    shift_ref,
    orb_ref,
    scale_ref,
    wave_ref,
    ham_ref,
    basis_ref,
    left,
    right,
    carried,
    zbuf,
    wall,
    mats,
    perm,
    basis_t,
    sig,
    rs_send,
    rs_recv,
    corr_own,
    corr_sib,
    corr_x,
    corr_zown,
    corr_z,
    zs_send,
    zs_recv,
    small_sem,
    load_sem,
    zsend_sem,
    zrecv_sem,
    xsend_sem,
    xrecv_sem,
    csend_sem,
    crecv_sem,
    rsend_sem,
    rrecv_sem,
    ksend_sem,
    krecv_sem,
    qsend_sem,
    qrecv_sem,
    ssend_sem,
    srecv_sem,
    tsend_sem,
    trecv_sem,
):
    ops = lax.axis_index("ops")
    sec = lax.axis_index("sec")
    z = ops // NJ
    j = ops % NJ
    x_hi = j // 4
    y = j % 4
    x_lo = sec // 2
    core = sec % 2
    x = x_hi * 2 + x_lo

    def at_z(i):
        return {"ops": ((z + i) % NZ) * NJ + j, "sec": sec}

    def place(a, b):
        px, py = (x + a) % 4, (y + b) % 4
        return (px // 2) * 4 + py, (px % 2) * 2 + core

    def at_plane(step):
        pj, psec = place(*step)
        return {"ops": z * NJ + pj, "sec": psec}

    def plane_slot(step):
        pj, psec = place(*step)
        return psec * NJ + pj

    def at_j(step):
        t = ((x_hi + step[0]) % 2) * 4 + (y + step[1]) % 4
        return t, {"ops": z * NJ + t, "sec": sec}

    sibling = {"ops": ops, "sec": x_lo * 2 + (1 - core)}

    def send(src, dst, send_sem, recv_sem, device):
        pltpu.make_async_remote_copy(
            src_ref=src,
            dst_ref=dst,
            send_sem=send_sem,
            recv_sem=recv_sem,
            device_id=device,
            device_id_type=MESH,
        ).start()

    def taken(ref, sem):
        pltpu.make_async_copy(ref, ref, sem).wait()

    sent = []

    def owe(ref, sem):
        sent.append(lambda: taken(ref, sem))

    barrier = pltpu.get_barrier_semaphore()
    for i in Z_STEPS:
        pl.semaphore_signal(barrier, inc=1, device_id=at_z(i), device_id_type=MESH)
    for step in XY_STEPS:
        pl.semaphore_signal(barrier, inc=1, device_id=at_plane(step), device_id_type=MESH)
    pl.semaphore_signal(barrier, inc=1, device_id=sibling, device_id_type=MESH)

    rows_in = (
        pltpu.make_async_copy(live_hbm, live_ref, small_sem.at[0]),
        pltpu.make_async_copy(wave_hbm, wave_ref, small_sem.at[1]),
        pltpu.make_async_copy(basis_hbm, basis_ref, small_sem.at[2]),
    )
    pairs_in = (
        pltpu.make_async_copy(ham_hbm, ham_ref, small_sem.at[3]),
        pltpu.make_async_copy(shift_hbm, shift_ref, small_sem.at[4]),
        pltpu.make_async_copy(orb_hbm, orb_ref, small_sem.at[5]),
        pltpu.make_async_copy(scale_hbm, scale_ref, small_sem.at[6]),
        pltpu.make_async_copy(right_hbm.at[0], right, load_sem.at[0]),
    )
    left_in = pltpu.make_async_copy(left_hbm.at[0], left, load_sem.at[1])
    for copy in rows_in + pairs_in + (left_in,):
        copy.start()

    m_ids = lax.broadcasted_iota(jnp.int32, (D, D), 0)
    s_ids = lax.broadcasted_iota(jnp.int32, (D, D), 1)
    wanted = ((m_ids % 16) // 2) * 32 + (m_ids % 2) * 16 + m_ids // 16
    perm[0] = jnp.where(wanted == s_ids, 1.0, 0.0).astype(BF16)
    perm[1] = jnp.where(m_ids == s_ids, 1.0, 0.0).astype(BF16)

    for copy in rows_in:
        copy.wait()
    live = live_ref[0, 0]
    row_ids = ops * 2 + lax.broadcasted_iota(jnp.int32, (2, D), 0)
    col_ids = lax.broadcasted_iota(jnp.int32, (2, D), 1)
    keep = (row_ids < live) & (col_ids < live)
    masked_rows = jnp.where(keep, wave_ref[0].astype(F32), 0.0)
    basis_rows = basis_ref[0].astype(F32)
    for w, rows in enumerate((masked_rows, basis_rows)):
        zbuf[w, z] = jnp.concatenate([rows[:, :H], rows[:, H:]], axis=0).astype(BF16)

    pl.semaphore_wait(barrier, (NZ - 1) + (NX - 1) + 1)

    for w in range(2):
        for i in Z_STEPS:
            send(zbuf.at[w, z], zbuf.at[w, z], zsend_sem.at[w], zrecv_sem.at[w], at_z(i))
        owe(zbuf.at[w, pl.ds(0, NZ - 1)], zsend_sem.at[w])

    slot = sec * NJ + j
    for w in range(2):
        taken(zbuf.at[w, pl.ds(0, NZ - 1)], zrecv_sem.at[w])
        pieces = zbuf[w].astype(F32)
        for h in range(2):
            for r in range(2):
                wall[w, slot, r * 16 : (r + 1) * 16, h * H : (h + 1) * H] = pieces[:, 2 * h + r, :].astype(BF16)
        for n, step in enumerate(XY_STEPS):
            send(
                wall.at[w, slot],
                wall.at[w, slot],
                xsend_sem.at[w],
                xrecv_sem.at[w, n],
                at_plane(step),
            )
        owe(wall.at[w, pl.ds(0, NX - 1)], xsend_sem.at[w])
        send(wall.at[w, slot], wall.at[w, slot], csend_sem.at[w], crecv_sem.at[w], sibling)

    def pass_on(w):
        for n in reversed(range(NX - 1)):
            a, b = XY_STEPS[n]
            s = plane_slot((4 - a, 4 - b))
            taken(wall.at[w, s], xrecv_sem.at[w, n])
            send(wall.at[w, s], wall.at[w, s], csend_sem.at[w], crecv_sem.at[w], sibling)
        owe(wall.at[w, pl.ds(0, NX)], csend_sem.at[w])

    def assemble(w):
        taken(wall.at[w, pl.ds(0, NX)], crecv_sem.at[w])
        for u in range(NSEC):
            stacked = wall[w, u * NJ : (u + 1) * NJ].reshape(D, D)
            mats[w, u] = nn(perm[0], stacked).astype(BF16)

    pass_on(0)
    assemble(0)

    for copy in pairs_in:
        copy.wait()

    def source(k):
        u = sec - shift_ref[k]
        inside = (u >= 0) & (u < NSEC)
        return jnp.clip(u, 0, NSEC - 1), inside

    for k in range(NPAIR):
        u, inside = source(k)
        weight = scale_ref[orb_ref[0, k]] * scale_ref[orb_ref[1, k]] * SCALE
        weight = jnp.where(inside, weight, 0.0)
        carried[k] = (weight * nt(mats[0, u], right[k])).astype(BF16)

    left_in.wait()
    total = nn(left[0], carried[0])
    for k in range(1, NPAIR):
        total += nn(left[k], carried[k])
    for h in range(2):
        sig[h] = total[:, h * H : (h + 1) * H]

    for t in range(NJ):
        for h in range(2):
            for r in range(2):
                rs_send[t, 2 * h + r] = sig[h, pl.ds(2 * t + r, 16, stride=16), :].astype(BF16)
    for step in J_STEPS:
        t, device = at_j(step)
        send(rs_send.at[t], rs_recv.at[j], rsend_sem, rrecv_sem, device)
    owe(rs_send.at[pl.ds(0, NJ - 1)], rsend_sem)
    rs_recv[j] = rs_send[j]

    own_wave = mats[0, sec]
    ham_rows = nn(ham_ref[0], own_wave)
    num = jnp.sum(ham_rows * masked_rows, axis=0, keepdims=True)
    lanes = num[:, :H] + num[:, H:]
    for h in range(2):
        wide = own_wave[:, h * H : (h + 1) * H].astype(F32)
        lanes += jnp.sum(sig[h] * wide, axis=0, keepdims=True)
    corr_own[...] = lanes
    send(corr_own, corr_sib, ksend_sem, krecv_sem, sibling)
    owe(corr_own, ksend_sem)

    pass_on(1)

    taken(corr_sib, krecv_sem)
    corr_x[x_lo * NJ + j] = corr_own[...] + corr_sib[...]
    for step in XY_STEPS:
        mine = corr_x.at[x_lo * NJ + j]
        send(mine, mine, qsend_sem, qrecv_sem, at_plane(step))
    owe(corr_x.at[pl.ds(0, NX - 1)], qsend_sem)

    assemble(1)
    basis_t[...] = nt(perm[1], mats[1, sec]).astype(BF16)

    def renormalize(ks):
        for k in ks:
            u, inside = source(k)
            left_basis = nn(left[k], mats[1, u]).astype(BF16)
            value = nn(basis_t[...], left_basis)
            renorm_ref[0, k] = jnp.where(inside, value, 0.0).astype(BF16)

    renormalize(range(NPAIR // 2))

    taken(rs_recv.at[pl.ds(0, NJ - 1)], rrecv_sem)
    chunk = [rs_recv[0, q].astype(F32) for q in range(4)]
    for t in range(1, NJ):
        for q in range(4):
            chunk[q] += rs_recv[t, q].astype(F32)
    for q in range(4):
        zs_send[:, q, :] = chunk[q]
    for i in Z_STEPS:
        send(zs_send.at[(z + i) % NZ], zs_recv.at[z], ssend_sem, srecv_sem, at_z(i))
    owe(zs_send.at[pl.ds(0, NZ - 1)], ssend_sem)

    taken(corr_x.at[pl.ds(0, NX - 1)], qrecv_sem)
    corr_zown[...] = jnp.sum(corr_x[...], axis=0)
    for i in Z_STEPS:
        send(corr_zown, corr_z.at[z], tsend_sem, trecv_sem, at_z(i))
    owe(corr_z.at[pl.ds(0, NZ - 1)], tsend_sem)
    zs_recv[z] = zs_send[z]
    corr_z[z] = corr_zown[...]

    renormalize(range(NPAIR // 2, NPAIR))

    norm = jnp.zeros((D, D), F32)
    for u in range(NSEC):
        wide = mats[0, u].astype(F32)
        norm += wide * wide
    norm = jnp.sum(jnp.sum(norm, axis=0, keepdims=True), axis=1, keepdims=True)

    taken(zs_recv.at[pl.ds(0, NZ - 1)], srecv_sem)
    summed = jnp.sum(zs_recv[...], axis=0)
    taken(corr_z.at[pl.ds(0, NZ - 1)], trecv_sem)
    energy = jnp.sum(jnp.sum(corr_z[...], axis=0), axis=1, keepdims=True) / norm
    for h in range(2):
        rows = summed[2 * h : 2 * h + 2, :] + ham_rows[:, h * H : (h + 1) * H]
        resid_ref[0, :, h * H : (h + 1) * H] = rows - energy * masked_rows[:, h * H : (h + 1) * H]

    for wait in sent:
        wait()


def on_device(
    wave,
    sector_live,
    left_ops,
    right_ops,
    pair_shift,
    pair_orbitals,
    orbital_scale,
    block_ham,
    site_basis,
):
    vmem = pl.BlockSpec(memory_space=pltpu.VMEM)
    hbm = pl.BlockSpec(memory_space=pltpu.HBM)
    dma = pltpu.SemaphoreType.DMA

    def in_hbm(value):
        return pltpu.with_memory_space_constraint(value, pltpu.HBM)

    return pl.pallas_call(
        kernel,
        out_shape=(
            jax.ShapeDtypeStruct((1, 2, D), F32),
            jax.ShapeDtypeStruct((1, NPAIR, D, D), BF16),
        ),
        in_specs=[hbm] * 9,
        out_specs=(vmem, vmem),
        scratch_shapes=[
            pltpu.SMEM((1, 1), jnp.int32),
            pltpu.SMEM((NPAIR,), jnp.int32),
            pltpu.SMEM((2, NPAIR), jnp.int32),
            pltpu.SMEM((NORB,), F32),
            pltpu.VMEM((1, 2, D), BF16),
            pltpu.VMEM((1, 2, D), BF16),
            pltpu.VMEM((1, 2, D), BF16),
            pltpu.VMEM((NPAIR, D, D), BF16),
            pltpu.VMEM((NPAIR, D, D), BF16),
            pltpu.VMEM((NPAIR, D, D), BF16),
            pltpu.VMEM((2, NZ, 4, H), BF16),
            pltpu.VMEM((2, NSEC * NJ, 32, D), BF16),
            pltpu.VMEM((2, NSEC, D, D), BF16),
            pltpu.VMEM((2, D, D), BF16),
            pltpu.VMEM((D, D), BF16),
            pltpu.VMEM((2, D, H), F32),
            pltpu.VMEM((NJ, 4, NZ, H), BF16),
            pltpu.VMEM((NJ, 4, NZ, H), BF16),
            pltpu.VMEM((1, H), F32),
            pltpu.VMEM((1, H), F32),
            pltpu.VMEM((NX, 1, H), F32),
            pltpu.VMEM((1, H), F32),
            pltpu.VMEM((NZ, 1, H), F32),
            pltpu.VMEM((NZ, 4, H), F32),
            pltpu.VMEM((NZ, 4, H), F32),
            dma((7,)),
            dma((2,)),
            dma((2,)),
            dma((2,)),
            dma((2,)),
            dma((2, NX)),
            dma((2,)),
            dma((2,)),
            dma,
            dma,
            dma,
            dma,
            dma,
            dma,
            dma,
            dma,
            dma,
            dma,
        ],
        compiler_params=pltpu.CompilerParams(
            collective_id=0, has_side_effects=True, vmem_limit_bytes=48 * 1024 * 1024
        ),
        cost_estimate=pl.CostEstimate(flops=1900000000, bytes_accessed=4800000, transcendentals=0),
    )(
        sector_live.reshape(1, 1),
        in_hbm(pair_shift),
        in_hbm(pair_orbitals.T),
        in_hbm(orbital_scale),
        in_hbm(wave),
        in_hbm(block_ham),
        in_hbm(site_basis),
        in_hbm(left_ops),
        in_hbm(right_ops),
    )


def solution(mesh):
    placed = (
        P("sec", "ops", None),
        P("sec"),
        P("sec", "ops", None, None),
        P("sec", "ops", None, None),
        P("ops"),
        P("ops", None),
        P(),
        P("sec", "ops", None),
        P("sec", "ops", None),
    )
    return jax.shard_map(
        on_device,
        mesh=mesh,
        in_specs=placed,
        out_specs=(P("sec", "ops", None), P("sec", "ops", None, None)),
        check_vma=False,
    )
```

```python
import functools
import math

import jax
import jax.numpy as jnp
from jax import lax
from jax.experimental import pallas as pl
from jax.experimental.pallas import tpu as pltpu
from jax.sharding import PartitionSpec as P

MESH = pl.DeviceIdType.MESH
F32 = jnp.float32
BF16 = jnp.bfloat16
NZ = 16
NJ = 8
NX = 16
NSEC = 4
NPAIR = 12
NORB = 120
D = 256
H = 128
SCALE = 1.0 / math.sqrt(256 * 1536)

NEAR = 4
DIRECT = {(0, 0): 1, (0, 1): 1, (1, 0): 1, (1, 1): 1}

Z_STEPS = sorted(range(1, NZ), key=lambda i: -min(i, NZ - i))
XY_STEPS = sorted(
    [(a, b) for a in range(4) for b in range(4) if a or b],
    key=lambda s: -(min(s[0], 4 - s[0]) + min(s[1], 4 - s[1])),
)
J_STEPS = sorted(
    [(a, b) for a in range(2) for b in range(4) if a or b],
    key=lambda s: -(2 * s[0] + min(s[1], 4 - s[1])),
)


def nt(a, b):
    return lax.dot_general(a, b, (((1,), (1,)), ((), ())), preferred_element_type=F32)


def nn(a, b):
    return jnp.dot(a, b, preferred_element_type=F32)


def kernel(
    live_hbm,
    shift_hbm,
    orb_hbm,
    scale_hbm,
    wave_hbm,
    ham_hbm,
    basis_hbm,
    left_hbm,
    right_hbm,
    resid_ref,
    renorm_ref,
    live_ref,
    shift_ref,
    orb_ref,
    scale_ref,
    wave_ref,
    ham_ref,
    basis_ref,
    left,
    right,
    carried,
    zbuf,
    wall_wave,
    wall_basis,
    mine,
    perm,
    basis_t,
    sig,
    rs_send,
    rs_recv,
    corr_x,
    corr_zown,
    corr_z,
    zs_send,
    zs_recv,
    small_sem,
    load_sem,
    zsend_sem,
    zrecv_sem,
    xsend_sem,
    osend_sem,
    xrecv_sem,
    csend_sem,
    crecv_sem,
    rsend_sem,
    rrecv_sem,
    qsend_sem,
    qrecv_sem,
    ssend_sem,
    srecv_sem,
    tsend_sem,
    trecv_sem,
):
    walls = (wall_wave, wall_basis)
    ops = lax.axis_index("ops")
    sec = lax.axis_index("sec")
    z = ops // NJ
    j = ops % NJ
    x_hi = j // 4
    y = j % 4
    x_lo = sec // 2
    core = sec % 2
    x = x_hi * 2 + x_lo

    def at_z(i):
        return {"ops": ((z + i) % NZ) * NJ + j, "sec": sec}

    def place(a, b):
        px, py = (x + a) % 4, (y + b) % 4
        return (px // 2) * 4 + py, (px % 2) * 2 + core

    def at_plane(step):
        pj, psec = place(*step)
        return {"ops": z * NJ + pj, "sec": psec}

    def at_plane_other(step):
        pj, psec = place(*step)
        return {"ops": z * NJ + pj, "sec": psec + 1 - 2 * core}

    def at_j(step):
        t = ((x_hi + step[0]) % 2) * 4 + (y + step[1]) % 4
        return t, {"ops": z * NJ + t, "sec": sec}

    sibling = {"ops": ops, "sec": x_lo * 2 + (1 - core)}

    def send(src, dst, send_sem, recv_sem, device):
        pltpu.make_async_remote_copy(
            src_ref=src,
            dst_ref=dst,
            send_sem=send_sem,
            recv_sem=recv_sem,
            device_id=device,
            device_id_type=MESH,
        ).start()

    def taken(ref, sem):
        pltpu.make_async_copy(ref, ref, sem).wait()

    sent = []

    def owe(ref, sem):
        sent.append(lambda: taken(ref, sem))

    barrier = pltpu.get_barrier_semaphore()
    greeted = [at_z(i) for d in range(NEAR, 0, -1) for i in (d, NZ - d)]
    greeted += [at_plane(step) for step in XY_STEPS] + [sibling]
    greeted += [at_plane_other(step) for step in XY_STEPS[: max(DIRECT.values())]]
    for device in greeted:
        pl.semaphore_signal(barrier, inc=1, device_id=device, device_id_type=MESH)

    rows_in = (
        pltpu.make_async_copy(live_hbm, live_ref, small_sem.at[0]),
        pltpu.make_async_copy(wave_hbm, wave_ref, small_sem.at[1]),
        pltpu.make_async_copy(basis_hbm, basis_ref, small_sem.at[2]),
    )
    pairs_in = (
        pltpu.make_async_copy(ham_hbm, ham_ref, small_sem.at[3]),
        pltpu.make_async_copy(shift_hbm, shift_ref, small_sem.at[4]),
        pltpu.make_async_copy(orb_hbm, orb_ref, small_sem.at[5]),
        pltpu.make_async_copy(scale_hbm, scale_ref, small_sem.at[6]),
        pltpu.make_async_copy(right_hbm.at[0], right, load_sem.at[0]),
    )
    left_in = pltpu.make_async_copy(left_hbm.at[0], left, load_sem.at[1])
    for copy in rows_in + pairs_in + (left_in,):
        copy.start()

    m_ids = lax.broadcasted_iota(jnp.int32, (D, D), 0)
    g_ids = lax.broadcasted_iota(jnp.int32, (D, D), 1)
    s_ids = lax.rem(m_ids // 16 + (NZ + NEAR) - z, NZ)
    wanted = (s_ids // 8) * 128 + ((m_ids % 16) // 2) * 16 + (m_ids % 2) * 8 + s_ids % 8
    perm[0] = jnp.where(wanted == g_ids, 1.0, 0.0).astype(BF16)
    perm[1] = jnp.where(m_ids == g_ids, 1.0, 0.0).astype(BF16)

    for copy in rows_in:
        copy.wait()
    live = live_ref[0, 0]
    row_ids = ops * 2 + lax.broadcasted_iota(jnp.int32, (2, D), 0)
    col_ids = lax.broadcasted_iota(jnp.int32, (2, D), 1)
    keep = (row_ids < live) & (col_ids < live)
    masked_rows = jnp.where(keep, wave_ref[0].astype(F32), 0.0)
    basis_rows = basis_ref[0].astype(F32)
    for w, rows in enumerate((masked_rows, basis_rows)):
        zbuf[w, NEAR] = jnp.concatenate([rows[:, :H], rows[:, H:]], axis=0).astype(BF16)

    pl.semaphore_wait(barrier, len(greeted))

    for w in range(2):
        for d in range(NEAR, 0, -1):
            send(zbuf.at[w, NEAR], zbuf.at[w, NEAR - d], zsend_sem.at[w], zrecv_sem.at[w, 0], at_z(d))
            send(zbuf.at[w, NEAR], zbuf.at[w, NEAR + d], zsend_sem.at[w], zrecv_sem.at[w, 0], at_z(NZ - d))
        owe(zbuf.at[w, pl.ds(0, NZ - 1)], zsend_sem.at[w])

    def relay(w):
        taken(zbuf.at[w, pl.ds(0, 2 * NEAR)], zrecv_sem.at[w, 0])
        send(
            zbuf.at[w, pl.ds(5, 4)], zbuf.at[w, pl.ds(9, 4)], zsend_sem.at[w], zrecv_sem.at[w, 1], at_z(NZ - NEAR)
        )
        send(
            zbuf.at[w, pl.ds(1, 3)], zbuf.at[w, pl.ds(13, 3)], zsend_sem.at[w], zrecv_sem.at[w, 1], at_z(NEAR)
        )

    def spread(w, half):
        if half == 1:
            taken(zbuf.at[w, pl.ds(9, 7)], zrecv_sem.at[w, 1])
        pieces = zbuf[w, 8 * half : 8 * half + 8].astype(F32)
        rows = [
            jnp.concatenate([pieces[:, r, :], pieces[:, 2 + r, :]], axis=1) for r in range(2)
        ]
        block = walls[w].at[sec, half, j]
        block[...] = jnp.concatenate(rows, axis=0).astype(BF16)
        n_direct = DIRECT[w, half]
        xs, os, cs = xsend_sem.at[w, half], osend_sem.at[w, half], csend_sem.at[w, half]
        for n, step in enumerate(XY_STEPS):
            send(block, block, xs, xrecv_sem.at[w, half, n], at_plane(step))
            if n < n_direct:
                send(block, block, os, crecv_sem.at[w, half], at_plane_other(step))
        send(block, block, cs, crecv_sem.at[w, half], sibling)
        owe(blocks(NX - 1), xs)
        owe(blocks(n_direct), os)
        owe(blocks(NX - n_direct), cs)

    def blocks(count):
        return right.at[0, pl.ds(0, 16 * count)]

    def pass_on(w, half):
        for n in reversed(range(NX - 1)):
            a, b = XY_STEPS[n]
            pj, psec = place(4 - a, 4 - b)
            block = walls[w].at[psec, half, pj]
            taken(block, xrecv_sem.at[w, half, n])
            if n >= DIRECT[w, half]:
                send(block, block, csend_sem.at[w, half], crecv_sem.at[w, half], sibling)

    def passed(w, half):
        taken(walls[w].at[pl.ds(0, 2), half], crecv_sem.at[w, half])

    def gathered(w, u):
        return walls[w][u].reshape(D, D)

    relay(0)
    spread(0, 0)
    relay(1)
    spread(1, 0)
    spread(0, 1)
    pass_on(0, 0)
    pass_on(1, 0)

    left_in.wait()
    for k in range(NPAIR):
        left[k] = nn(left[k], perm[0]).astype(BF16)

    pass_on(0, 1)
    spread(1, 1)
    passed(0, 0)
    passed(0, 1)

    for copy in pairs_in:
        copy.wait()

    def source(k):
        u = sec - shift_ref[k]
        inside = (u >= 0) & (u < NSEC)
        return jnp.clip(u, 0, NSEC - 1), inside

    for k in range(NPAIR):
        u, inside = source(k)
        weight = scale_ref[orb_ref[0, k]] * scale_ref[orb_ref[1, k]] * SCALE
        weight = jnp.where(inside, weight, 0.0)
        carried[k] = (weight * nt(gathered(0, u), right[k])).astype(BF16)

    total = nn(left[0], carried[0])
    for k in range(1, NPAIR):
        total += nn(left[k], carried[k])
    for h in range(2):
        sig[h] = total[:, h * H : (h + 1) * H]

    for t in range(NJ):
        for h in range(2):
            for r in range(2):
                rs_send[t, 2 * h + r] = sig[h, pl.ds(2 * t + r, 16, stride=16), :].astype(BF16)
    for step in J_STEPS:
        t, device = at_j(step)
        send(rs_send.at[t], rs_recv.at[j], rsend_sem, rrecv_sem, device)
    owe(rs_send.at[pl.ds(0, NJ - 1)], rsend_sem)
    rs_recv[j] = rs_send[j]

    own_wave = nn(perm[0], gathered(0, sec)).astype(BF16)
    ham_rows = nn(ham_ref[0], own_wave)
    num = jnp.sum(ham_rows * masked_rows, axis=0, keepdims=True)
    lanes = num[:, :H] + num[:, H:]
    for h in range(2):
        wide = own_wave[:, h * H : (h + 1) * H].astype(F32)
        lanes += jnp.sum(sig[h] * wide, axis=0, keepdims=True)
    place_own = sec * NJ + j
    corr_x[place_own] = lanes
    part = corr_x.at[place_own]
    for step in XY_STEPS:
        send(part, part, qsend_sem, qrecv_sem, at_plane_other(step))
        send(part, part, qsend_sem, qrecv_sem, at_plane(step))
    send(part, part, qsend_sem, qrecv_sem, sibling)
    owe(corr_x.at[pl.ds(0, 2 * NX - 1)], qsend_sem)

    def renormalize(ks):
        for k in ks:
            u, inside = source(k)
            left_basis = nn(left[k], gathered(1, u)).astype(BF16)
            value = nn(basis_t[...], left_basis)
            renorm_ref[0, k] = jnp.where(inside, value, 0.0).astype(BF16)

    norm = jnp.zeros((D, D), F32)
    for u in range(NSEC):
        wide = gathered(0, u).astype(F32)
        norm += wide * wide
    norm = jnp.sum(jnp.sum(norm, axis=0, keepdims=True), axis=1, keepdims=True)

    taken(rs_recv.at[pl.ds(0, NJ - 1)], rrecv_sem)
    chunk = [rs_recv[0, q].astype(F32) for q in range(4)]
    for t in range(1, NJ):
        for q in range(4):
            chunk[q] += rs_recv[t, q].astype(F32)
    for q in range(4):
        zs_send[:, q, :] = chunk[q]
    for i in Z_STEPS:
        send(zs_send.at[(z + i) % NZ], zs_recv.at[z], ssend_sem, srecv_sem, at_z(i))
    owe(zs_send.at[pl.ds(0, NZ - 1)], ssend_sem)

    taken(corr_x.at[pl.ds(0, 2 * NX - 1)], qrecv_sem)
    corr_zown[...] = jnp.sum(corr_x[...], axis=0)
    for i in Z_STEPS:
        send(corr_zown, corr_z.at[z], tsend_sem, trecv_sem, at_z(i))
    owe(corr_z.at[pl.ds(0, NZ - 1)], tsend_sem)
    zs_recv[z] = zs_send[z]
    corr_z[z] = corr_zown[...]

    pass_on(1, 1)
    passed(1, 0)
    passed(1, 1)
    mine[...] = nn(perm[0], gathered(1, sec)).astype(BF16)
    basis_t[...] = nt(perm[1], mine[...]).astype(BF16)

    renormalize(range(NPAIR))

    taken(zs_recv.at[pl.ds(0, NZ - 1)], srecv_sem)
    summed = jnp.sum(zs_recv[...], axis=0)
    taken(corr_z.at[pl.ds(0, NZ - 1)], trecv_sem)
    energy = jnp.sum(jnp.sum(corr_z[...], axis=0), axis=1, keepdims=True) / norm
    for h in range(2):
        rows = summed[2 * h : 2 * h + 2, :] + ham_rows[:, h * H : (h + 1) * H]
        resid_ref[0, :, h * H : (h + 1) * H] = rows - energy * masked_rows[:, h * H : (h + 1) * H]

    for wait in sent:
        wait()


def on_device(
    wave,
    sector_live,
    left_ops,
    right_ops,
    pair_shift,
    pair_orbitals,
    orbital_scale,
    block_ham,
    site_basis,
):
    vmem = pl.BlockSpec(memory_space=pltpu.VMEM)
    hbm = pl.BlockSpec(memory_space=pltpu.HBM)
    dma = pltpu.SemaphoreType.DMA

    def in_hbm(value):
        return pltpu.with_memory_space_constraint(value, pltpu.HBM)

    return pl.pallas_call(
        kernel,
        out_shape=(
            jax.ShapeDtypeStruct((1, 2, D), F32),
            jax.ShapeDtypeStruct((1, NPAIR, D, D), BF16),
        ),
        in_specs=[hbm] * 9,
        out_specs=(vmem, vmem),
        scratch_shapes=[
            pltpu.SMEM((1, 1), jnp.int32),
            pltpu.SMEM((NPAIR,), jnp.int32),
            pltpu.SMEM((2, NPAIR), jnp.int32),
            pltpu.SMEM((NORB,), F32),
            pltpu.VMEM((1, 2, D), BF16),
            pltpu.VMEM((1, 2, D), BF16),
            pltpu.VMEM((1, 2, D), BF16),
            pltpu.VMEM((NPAIR, D, D), BF16),
            pltpu.VMEM((NPAIR, D, D), BF16),
            pltpu.VMEM((NPAIR, D, D), BF16),
            pltpu.VMEM((2, NZ, 4, H), BF16),
            pltpu.VMEM((NSEC, 2, NJ, 16, D), BF16),
            pltpu.VMEM((NSEC, 2, NJ, 16, D), BF16),
            pltpu.VMEM((D, D), BF16),
            pltpu.VMEM((2, D, D), BF16),
            pltpu.VMEM((D, D), BF16),
            pltpu.VMEM((2, D, H), F32),
            pltpu.VMEM((NJ, 4, NZ, H), BF16),
            pltpu.VMEM((NJ, 4, NZ, H), BF16),
            pltpu.VMEM((2 * NX, 1, H), F32),
            pltpu.VMEM((1, H), F32),
            pltpu.VMEM((NZ, 1, H), F32),
            pltpu.VMEM((NZ, 4, H), F32),
            pltpu.VMEM((NZ, 4, H), F32),
            dma((7,)),
            dma((2,)),
            dma((2,)),
            dma((2, 2)),
            dma((2, 2)),
            dma((2, 2)),
            dma((2, 2, NX)),
            dma((2, 2)),
            dma((2, 2)),
            dma,
            dma,
            dma,
            dma,
            dma,
            dma,
            dma,
            dma,
        ],
        compiler_params=pltpu.CompilerParams(
            collective_id=0, has_side_effects=True, vmem_limit_bytes=48 * 1024 * 1024
        ),
        cost_estimate=pl.CostEstimate(flops=1900000000, bytes_accessed=4800000, transcendentals=0),
    )(
        sector_live.reshape(1, 1),
        in_hbm(pair_shift),
        in_hbm(pair_orbitals.T),
        in_hbm(orbital_scale),
        in_hbm(wave),
        in_hbm(block_ham),
        in_hbm(site_basis),
        in_hbm(left_ops),
        in_hbm(right_ops),
    )


def solution(mesh):
    placed = (
        P("sec", "ops", None),
        P("sec"),
        P("sec", "ops", None, None),
        P("sec", "ops", None, None),
        P("ops"),
        P("ops", None),
        P(),
        P("sec", "ops", None),
        P("sec", "ops", None),
    )
    return jax.shard_map(
        on_device,
        mesh=mesh,
        in_specs=placed,
        out_specs=(P("sec", "ops", None), P("sec", "ops", None, None)),
        check_vma=False,
    )
```

```python
import functools
import math

import jax
import jax.numpy as jnp
from jax import lax
from jax.experimental import pallas as pl
from jax.experimental.pallas import tpu as pltpu
from jax.sharding import PartitionSpec as P

MESH = pl.DeviceIdType.MESH
F32 = jnp.float32
BF16 = jnp.bfloat16
NZ = 16
NJ = 8
NX = 16
NSEC = 4
NPAIR = 12
NORB = 120
D = 256
H = 128
SCALE = 1.0 / math.sqrt(256 * 1536)

NEAR = 4
DIRECT = {(0, 0): 1, (0, 1): 1, (1, 0): 1, (1, 1): 1}

Z_STEPS = sorted(range(1, NZ), key=lambda i: -min(i, NZ - i))
XY_STEPS = sorted(
    [(a, b) for a in range(4) for b in range(4) if a or b],
    key=lambda s: -(min(s[0], 4 - s[0]) + min(s[1], 4 - s[1])),
)
J_STEPS = sorted(
    [(a, b) for a in range(2) for b in range(4) if a or b],
    key=lambda s: -(2 * s[0] + min(s[1], 4 - s[1])),
)


def nt(a, b):
    return lax.dot_general(a, b, (((1,), (1,)), ((), ())), preferred_element_type=F32)


def nn(a, b):
    return jnp.dot(a, b, preferred_element_type=F32)


def kernel(
    live_hbm,
    shift_hbm,
    orb_hbm,
    scale_hbm,
    wave_hbm,
    ham_hbm,
    basis_hbm,
    left_hbm,
    right_hbm,
    resid_ref,
    renorm_ref,
    live_ref,
    shift_ref,
    orb_ref,
    scale_ref,
    wave_ref,
    ham_ref,
    basis_ref,
    left,
    right,
    left_near,
    left_far,
    carried_near,
    carried_far,
    zbuf,
    wall_wave_near,
    wall_wave_far,
    wall_basis_near,
    wall_basis_far,
    mats,
    perm,
    basis_t,
    sig,
    rs_send,
    rs_recv,
    corr_x,
    corr_zown,
    corr_z,
    zs_send,
    zs_recv,
    small_sem,
    load_sem,
    zsend_sem,
    zrecv_sem,
    xsend_sem,
    osend_sem,
    xrecv_sem,
    csend_sem,
    crecv_sem,
    rsend_sem,
    rrecv_sem,
    qsend_sem,
    qrecv_sem,
    ssend_sem,
    srecv_sem,
    tsend_sem,
    trecv_sem,
):
    walls = ((wall_wave_near, wall_wave_far), (wall_basis_near, wall_basis_far))
    ops = lax.axis_index("ops")
    sec = lax.axis_index("sec")
    z = ops // NJ
    j = ops % NJ
    x_hi = j // 4
    y = j % 4
    x_lo = sec // 2
    core = sec % 2
    x = x_hi * 2 + x_lo

    def at_z(i):
        return {"ops": ((z + i) % NZ) * NJ + j, "sec": sec}

    def place(a, b):
        px, py = (x + a) % 4, (y + b) % 4
        return (px // 2) * 4 + py, (px % 2) * 2 + core

    def at_plane(step):
        pj, psec = place(*step)
        return {"ops": z * NJ + pj, "sec": psec}

    def at_plane_other(step):
        pj, psec = place(*step)
        return {"ops": z * NJ + pj, "sec": psec + 1 - 2 * core}

    def at_j(step):
        t = ((x_hi + step[0]) % 2) * 4 + (y + step[1]) % 4
        return t, {"ops": z * NJ + t, "sec": sec}

    sibling = {"ops": ops, "sec": x_lo * 2 + (1 - core)}

    def send(src, dst, send_sem, recv_sem, device):
        pltpu.make_async_remote_copy(
            src_ref=src,
            dst_ref=dst,
            send_sem=send_sem,
            recv_sem=recv_sem,
            device_id=device,
            device_id_type=MESH,
        ).start()

    def taken(ref, sem):
        pltpu.make_async_copy(ref, ref, sem).wait()

    sent = []

    def owe(ref, sem):
        sent.append(lambda: taken(ref, sem))

    barrier = pltpu.get_barrier_semaphore()
    greeted = [at_z(i) for d in range(NEAR, 0, -1) for i in (d, NZ - d)]
    greeted += [at_plane(step) for step in XY_STEPS] + [sibling]
    greeted += [at_plane_other(step) for step in XY_STEPS[: max(DIRECT.values())]]
    for device in greeted:
        pl.semaphore_signal(barrier, inc=1, device_id=device, device_id_type=MESH)

    rows_in = (
        pltpu.make_async_copy(live_hbm, live_ref, small_sem.at[0]),
        pltpu.make_async_copy(wave_hbm, wave_ref, small_sem.at[1]),
        pltpu.make_async_copy(basis_hbm, basis_ref, small_sem.at[2]),
    )
    pairs_in = (
        pltpu.make_async_copy(ham_hbm, ham_ref, small_sem.at[3]),
        pltpu.make_async_copy(shift_hbm, shift_ref, small_sem.at[4]),
        pltpu.make_async_copy(orb_hbm, orb_ref, small_sem.at[5]),
        pltpu.make_async_copy(scale_hbm, scale_ref, small_sem.at[6]),
        pltpu.make_async_copy(right_hbm.at[0], right, load_sem.at[0]),
    )
    left_in = pltpu.make_async_copy(left_hbm.at[0], left, load_sem.at[1])
    for copy in rows_in + pairs_in + (left_in,):
        copy.start()

    m_ids = lax.broadcasted_iota(jnp.int32, (D, D), 0)
    g_ids = lax.broadcasted_iota(jnp.int32, (D, D), 1)
    s_ids = lax.rem(m_ids // 16 + (NZ + NEAR) - z, NZ)
    wanted = (s_ids // 8) * 128 + ((m_ids % 16) // 2) * 16 + (m_ids % 2) * 8 + s_ids % 8
    perm[0] = jnp.where(wanted == g_ids, 1.0, 0.0).astype(BF16)
    perm[1] = jnp.where(m_ids == g_ids, 1.0, 0.0).astype(BF16)

    for copy in rows_in:
        copy.wait()
    live = live_ref[0, 0]
    row_ids = ops * 2 + lax.broadcasted_iota(jnp.int32, (2, D), 0)
    col_ids = lax.broadcasted_iota(jnp.int32, (2, D), 1)
    keep = (row_ids < live) & (col_ids < live)
    masked_rows = jnp.where(keep, wave_ref[0].astype(F32), 0.0)
    basis_rows = basis_ref[0].astype(F32)
    for w, rows in enumerate((masked_rows, basis_rows)):
        zbuf[w, NEAR] = jnp.concatenate([rows[:, :H], rows[:, H:]], axis=0).astype(BF16)

    pl.semaphore_wait(barrier, len(greeted))

    for w in range(2):
        for d in range(NEAR, 0, -1):
            send(zbuf.at[w, NEAR], zbuf.at[w, NEAR - d], zsend_sem.at[w], zrecv_sem.at[w, 0], at_z(d))
            send(zbuf.at[w, NEAR], zbuf.at[w, NEAR + d], zsend_sem.at[w], zrecv_sem.at[w, 0], at_z(NZ - d))
        owe(zbuf.at[w, pl.ds(0, NZ - 1)], zsend_sem.at[w])

    def relay(w):
        taken(zbuf.at[w, pl.ds(0, 2 * NEAR)], zrecv_sem.at[w, 0])
        send(
            zbuf.at[w, pl.ds(5, 4)], zbuf.at[w, pl.ds(9, 4)], zsend_sem.at[w], zrecv_sem.at[w, 1], at_z(NZ - NEAR)
        )
        send(
            zbuf.at[w, pl.ds(1, 3)], zbuf.at[w, pl.ds(13, 3)], zsend_sem.at[w], zrecv_sem.at[w, 1], at_z(NEAR)
        )

    def spread(w, half):
        if half == 1:
            taken(zbuf.at[w, pl.ds(9, 7)], zrecv_sem.at[w, 1])
        pieces = zbuf[w, 8 * half : 8 * half + 8].astype(F32)
        rows = [
            jnp.concatenate([pieces[:, r, :], pieces[:, 2 + r, :]], axis=1) for r in range(2)
        ]
        block = walls[w][half].at[sec, j]
        block[...] = jnp.concatenate(rows, axis=0).astype(BF16)
        n_direct = DIRECT[w, half]
        xs, os, cs = xsend_sem.at[w, half], osend_sem.at[w, half], csend_sem.at[w, half]
        for n, step in enumerate(XY_STEPS):
            send(block, block, xs, xrecv_sem.at[w, half, n], at_plane(step))
            if n < n_direct:
                send(block, block, os, crecv_sem.at[w, half], at_plane_other(step))
        send(block, block, cs, crecv_sem.at[w, half], sibling)
        owe(blocks(NX - 1), xs)
        owe(blocks(n_direct), os)
        owe(blocks(NX - n_direct), cs)

    def blocks(count):
        return right.at[0, pl.ds(0, 16 * count)]

    def pass_on(w, half):
        for n in reversed(range(NX - 1)):
            a, b = XY_STEPS[n]
            pj, psec = place(4 - a, 4 - b)
            block = walls[w][half].at[psec, pj]
            taken(block, xrecv_sem.at[w, half, n])
            if n >= DIRECT[w, half]:
                send(block, block, csend_sem.at[w, half], crecv_sem.at[w, half], sibling)

    def passed(w, half):
        taken(walls[w][half].at[pl.ds(0, 2)], crecv_sem.at[w, half])

    def gathered_half(w, half, u):
        return walls[w][half][u].reshape(H, D)

    def gathered(w, u):
        return jnp.concatenate([gathered_half(w, half, u) for half in range(2)], axis=0)

    relay(0)
    spread(0, 0)
    relay(1)
    spread(1, 0)
    spread(0, 1)
    pass_on(0, 0)
    pass_on(1, 0)

    left_in.wait()
    for k in range(NPAIR):
        columns = nn(left[k], perm[0]).astype(BF16)
        left_near[:, k * H : (k + 1) * H] = columns[:, :H]
        left_far[:, k * H : (k + 1) * H] = columns[:, H:]

    for copy in pairs_in:
        copy.wait()

    def source(k):
        u = sec - shift_ref[k]
        inside = (u >= 0) & (u < NSEC)
        return jnp.clip(u, 0, NSEC - 1), inside

    def pair_terms(half, left_part, carried_part):
        for k in range(NPAIR):
            u, inside = source(k)
            weight = scale_ref[orb_ref[0, k]] * scale_ref[orb_ref[1, k]] * SCALE
            weight = jnp.where(inside, weight, 0.0)
            product = nt(gathered_half(0, half, u), right[k])
            carried_part[k * H : (k + 1) * H, :] = (weight * product).astype(BF16)
        return nn(left_part[...], carried_part[...])

    passed(0, 0)
    total = pair_terms(0, left_near, carried_near)
    for h in range(2):
        sig[h] = total[:, h * H : (h + 1) * H]

    pass_on(0, 1)
    spread(1, 1)
    passed(0, 1)
    total = pair_terms(1, left_far, carried_far)
    for h in range(2):
        sig[h] += total[:, h * H : (h + 1) * H]

    for t in range(NJ):
        for h in range(2):
            for r in range(2):
                rs_send[t, 2 * h + r] = sig[h, pl.ds(2 * t + r, 16, stride=16), :].astype(BF16)
    for step in J_STEPS:
        t, device = at_j(step)
        send(rs_send.at[t], rs_recv.at[j], rsend_sem, rrecv_sem, device)
    owe(rs_send.at[pl.ds(0, NJ - 1)], rsend_sem)
    rs_recv[j] = rs_send[j]

    own_wave = nn(perm[0], gathered(0, sec)).astype(BF16)
    ham_rows = nn(ham_ref[0], own_wave)
    num = jnp.sum(ham_rows * masked_rows, axis=0, keepdims=True)
    lanes = num[:, :H] + num[:, H:]
    for h in range(2):
        wide = own_wave[:, h * H : (h + 1) * H].astype(F32)
        lanes += jnp.sum(sig[h] * wide, axis=0, keepdims=True)
    place_own = sec * NJ + j
    corr_x[place_own] = lanes
    part = corr_x.at[place_own]
    for step in XY_STEPS:
        send(part, part, qsend_sem, qrecv_sem, at_plane_other(step))
        send(part, part, qsend_sem, qrecv_sem, at_plane(step))
    send(part, part, qsend_sem, qrecv_sem, sibling)
    owe(corr_x.at[pl.ds(0, 2 * NX - 1)], qsend_sem)

    def renormalize(ks):
        for k in ks:
            u, inside = source(k)
            left_basis = nn(left[k], mats[u]).astype(BF16)
            value = nn(basis_t[...], left_basis)
            renorm_ref[0, k] = jnp.where(inside, value, 0.0).astype(BF16)

    norm = jnp.zeros((D, D), F32)
    for u in range(NSEC):
        wide = gathered(0, u).astype(F32)
        norm += wide * wide
    norm = jnp.sum(jnp.sum(norm, axis=0, keepdims=True), axis=1, keepdims=True)

    taken(rs_recv.at[pl.ds(0, NJ - 1)], rrecv_sem)
    chunk = [rs_recv[0, q].astype(F32) for q in range(4)]
    for t in range(1, NJ):
        for q in range(4):
            chunk[q] += rs_recv[t, q].astype(F32)
    for q in range(4):
        zs_send[:, q, :] = chunk[q]
    for i in Z_STEPS:
        send(zs_send.at[(z + i) % NZ], zs_recv.at[z], ssend_sem, srecv_sem, at_z(i))
    owe(zs_send.at[pl.ds(0, NZ - 1)], ssend_sem)

    taken(corr_x.at[pl.ds(0, 2 * NX - 1)], qrecv_sem)
    corr_zown[...] = jnp.sum(corr_x[...], axis=0)
    for i in Z_STEPS:
        send(corr_zown, corr_z.at[z], tsend_sem, trecv_sem, at_z(i))
    owe(corr_z.at[pl.ds(0, NZ - 1)], tsend_sem)
    zs_recv[z] = zs_send[z]
    corr_z[z] = corr_zown[...]

    pass_on(1, 1)
    passed(1, 0)
    passed(1, 1)
    for u in range(NSEC):
        mats[u] = nn(perm[0], gathered(1, u)).astype(BF16)
    basis_t[...] = nt(perm[1], mats[sec]).astype(BF16)

    renormalize(range(NPAIR))

    taken(zs_recv.at[pl.ds(0, NZ - 1)], srecv_sem)
    summed = jnp.sum(zs_recv[...], axis=0)
    taken(corr_z.at[pl.ds(0, NZ - 1)], trecv_sem)
    energy = jnp.sum(jnp.sum(corr_z[...], axis=0), axis=1, keepdims=True) / norm
    for h in range(2):
        rows = summed[2 * h : 2 * h + 2, :] + ham_rows[:, h * H : (h + 1) * H]
        resid_ref[0, :, h * H : (h + 1) * H] = rows - energy * masked_rows[:, h * H : (h + 1) * H]

    for wait in sent:
        wait()


def on_device(
    wave,
    sector_live,
    left_ops,
    right_ops,
    pair_shift,
    pair_orbitals,
    orbital_scale,
    block_ham,
    site_basis,
):
    vmem = pl.BlockSpec(memory_space=pltpu.VMEM)
    hbm = pl.BlockSpec(memory_space=pltpu.HBM)
    dma = pltpu.SemaphoreType.DMA

    def in_hbm(value):
        return pltpu.with_memory_space_constraint(value, pltpu.HBM)

    return pl.pallas_call(
        kernel,
        out_shape=(
            jax.ShapeDtypeStruct((1, 2, D), F32),
            jax.ShapeDtypeStruct((1, NPAIR, D, D), BF16),
        ),
        in_specs=[hbm] * 9,
        out_specs=(vmem, vmem),
        scratch_shapes=[
            pltpu.SMEM((1, 1), jnp.int32),
            pltpu.SMEM((NPAIR,), jnp.int32),
            pltpu.SMEM((2, NPAIR), jnp.int32),
            pltpu.SMEM((NORB,), F32),
            pltpu.VMEM((1, 2, D), BF16),
            pltpu.VMEM((1, 2, D), BF16),
            pltpu.VMEM((1, 2, D), BF16),
            pltpu.VMEM((NPAIR, D, D), BF16),
            pltpu.VMEM((NPAIR, D, D), BF16),
            pltpu.VMEM((D, NPAIR * H), BF16),
            pltpu.VMEM((D, NPAIR * H), BF16),
            pltpu.VMEM((NPAIR * H, D), BF16),
            pltpu.VMEM((NPAIR * H, D), BF16),
            pltpu.VMEM((2, NZ, 4, H), BF16),
            pltpu.VMEM((NSEC, NJ, 16, D), BF16),
            pltpu.VMEM((NSEC, NJ, 16, D), BF16),
            pltpu.VMEM((NSEC, NJ, 16, D), BF16),
            pltpu.VMEM((NSEC, NJ, 16, D), BF16),
            pltpu.VMEM((NSEC, D, D), BF16),
            pltpu.VMEM((2, D, D), BF16),
            pltpu.VMEM((D, D), BF16),
            pltpu.VMEM((2, D, H), F32),
            pltpu.VMEM((NJ, 4, NZ, H), BF16),
            pltpu.VMEM((NJ, 4, NZ, H), BF16),
            pltpu.VMEM((2 * NX, 1, H), F32),
            pltpu.VMEM((1, H), F32),
            pltpu.VMEM((NZ, 1, H), F32),
            pltpu.VMEM((NZ, 4, H), F32),
            pltpu.VMEM((NZ, 4, H), F32),
            dma((7,)),
            dma((2,)),
            dma((2,)),
            dma((2, 2)),
            dma((2, 2)),
            dma((2, 2)),
            dma((2, 2, NX)),
            dma((2, 2)),
            dma((2, 2)),
            dma,
            dma,
            dma,
            dma,
            dma,
            dma,
            dma,
            dma,
        ],
        compiler_params=pltpu.CompilerParams(
            collective_id=0, has_side_effects=True, vmem_limit_bytes=48 * 1024 * 1024
        ),
        cost_estimate=pl.CostEstimate(flops=1900000000, bytes_accessed=4800000, transcendentals=0),
    )(
        sector_live.reshape(1, 1),
        in_hbm(pair_shift),
        in_hbm(pair_orbitals.T),
        in_hbm(orbital_scale),
        in_hbm(wave),
        in_hbm(block_ham),
        in_hbm(site_basis),
        in_hbm(left_ops),
        in_hbm(right_ops),
    )


def solution(mesh):
    placed = (
        P("sec", "ops", None),
        P("sec"),
        P("sec", "ops", None, None),
        P("sec", "ops", None, None),
        P("ops"),
        P("ops", None),
        P(),
        P("sec", "ops", None),
        P("sec", "ops", None),
    )
    return jax.shard_map(
        on_device,
        mesh=mesh,
        in_specs=placed,
        out_specs=(P("sec", "ops", None), P("sec", "ops", None, None)),
        check_vma=False,
    )
```

```python
import functools
import math

import jax
import jax.numpy as jnp
from jax import lax
from jax.experimental import pallas as pl
from jax.experimental.pallas import tpu as pltpu
from jax.sharding import PartitionSpec as P

MESH = pl.DeviceIdType.MESH
F32 = jnp.float32
BF16 = jnp.bfloat16
NZ = 16
NJ = 8
NX = 16
NSEC = 4
NPAIR = 12
NORB = 120
D = 256
H = 128
SCALE = 1.0 / math.sqrt(256 * 1536)

NEAR = 4
DIRECT = {(0, 0): 1, (0, 1): 1, (1, 0): 1, (1, 1): 1}

Z_STEPS = sorted(range(1, NZ), key=lambda i: -min(i, NZ - i))
XY_STEPS = sorted(
    [(a, b) for a in range(4) for b in range(4) if a or b],
    key=lambda s: -(min(s[0], 4 - s[0]) + min(s[1], 4 - s[1])),
)
J_STEPS = sorted(
    [(a, b) for a in range(2) for b in range(4) if a or b],
    key=lambda s: -(2 * s[0] + min(s[1], 4 - s[1])),
)


def nt(a, b):
    return lax.dot_general(a, b, (((1,), (1,)), ((), ())), preferred_element_type=F32)


def nn(a, b):
    return jnp.dot(a, b, preferred_element_type=F32)


def kernel(
    live_hbm,
    shift_hbm,
    orb_hbm,
    scale_hbm,
    wave_hbm,
    ham_hbm,
    basis_hbm,
    left_hbm,
    right_hbm,
    resid_ref,
    renorm_ref,
    live_ref,
    shift_ref,
    orb_ref,
    scale_ref,
    wave_ref,
    ham_ref,
    basis_ref,
    left,
    right,
    left_near,
    left_far,
    carried_near,
    carried_far,
    zbuf,
    wall_wave_near,
    wall_wave_far,
    wall_basis_near,
    wall_basis_far,
    mats,
    perm,
    basis_t,
    sig,
    rs_send,
    rs_recv,
    corr_x,
    corr_zown,
    corr_z,
    zs_send,
    zs_recv,
    small_sem,
    load_sem,
    zsend_sem,
    zrecv_sem,
    xsend_sem,
    osend_sem,
    xrecv_sem,
    csend_sem,
    crecv_sem,
    rsend_sem,
    rrecv_sem,
    qsend_sem,
    qrecv_sem,
    ssend_sem,
    srecv_sem,
    tsend_sem,
    trecv_sem,
):
    walls = ((wall_wave_near, wall_wave_far), (wall_basis_near, wall_basis_far))
    ops = lax.axis_index("ops")
    sec = lax.axis_index("sec")
    z = ops // NJ
    j = ops % NJ
    x_hi = j // 4
    y = j % 4
    x_lo = sec // 2
    core = sec % 2
    x = x_hi * 2 + x_lo

    def at_z(i):
        return {"ops": ((z + i) % NZ) * NJ + j, "sec": sec}

    def place(a, b):
        px, py = (x + a) % 4, (y + b) % 4
        return (px // 2) * 4 + py, (px % 2) * 2 + core

    def at_plane(step):
        pj, psec = place(*step)
        return {"ops": z * NJ + pj, "sec": psec}

    def at_plane_other(step):
        pj, psec = place(*step)
        return {"ops": z * NJ + pj, "sec": psec + 1 - 2 * core}

    def at_j(step):
        t = ((x_hi + step[0]) % 2) * 4 + (y + step[1]) % 4
        return t, {"ops": z * NJ + t, "sec": sec}

    sibling = {"ops": ops, "sec": x_lo * 2 + (1 - core)}

    def send(src, dst, send_sem, recv_sem, device):
        pltpu.make_async_remote_copy(
            src_ref=src,
            dst_ref=dst,
            send_sem=send_sem,
            recv_sem=recv_sem,
            device_id=device,
            device_id_type=MESH,
        ).start()

    def taken(ref, sem):
        pltpu.make_async_copy(ref, ref, sem).wait()

    sent = []

    def owe(ref, sem):
        sent.append(lambda: taken(ref, sem))

    barrier = pltpu.get_barrier_semaphore()
    greeted = [at_z(i) for d in range(NEAR, 0, -1) for i in (d, NZ - d)]
    greeted += [at_plane(step) for step in XY_STEPS] + [sibling]
    greeted += [at_plane_other(step) for step in XY_STEPS[: max(DIRECT.values())]]
    for device in greeted:
        pl.semaphore_signal(barrier, inc=1, device_id=device, device_id_type=MESH)

    rows_in = (
        pltpu.make_async_copy(live_hbm, live_ref, small_sem.at[0]),
        pltpu.make_async_copy(wave_hbm, wave_ref, small_sem.at[1]),
        pltpu.make_async_copy(basis_hbm, basis_ref, small_sem.at[2]),
    )
    pairs_in = (
        pltpu.make_async_copy(ham_hbm, ham_ref, small_sem.at[3]),
        pltpu.make_async_copy(shift_hbm, shift_ref, small_sem.at[4]),
        pltpu.make_async_copy(orb_hbm, orb_ref, small_sem.at[5]),
        pltpu.make_async_copy(scale_hbm, scale_ref, small_sem.at[6]),
        pltpu.make_async_copy(right_hbm.at[0], right, load_sem.at[0]),
    )
    left_in = pltpu.make_async_copy(left_hbm.at[0], left, load_sem.at[1])
    for copy in rows_in + pairs_in + (left_in,):
        copy.start()

    m_ids = lax.broadcasted_iota(jnp.int32, (D, D), 0)
    g_ids = lax.broadcasted_iota(jnp.int32, (D, D), 1)
    s_ids = lax.rem(m_ids // 16 + (NZ + NEAR) - z, NZ)
    wanted = (s_ids // 8) * 128 + ((m_ids % 16) // 2) * 16 + (m_ids % 2) * 8 + s_ids % 8
    perm[0] = jnp.where(wanted == g_ids, 1.0, 0.0).astype(BF16)
    perm[1] = jnp.where(m_ids == g_ids, 1.0, 0.0).astype(BF16)

    for copy in rows_in:
        copy.wait()
    live = live_ref[0, 0]
    row_ids = ops * 2 + lax.broadcasted_iota(jnp.int32, (2, D), 0)
    col_ids = lax.broadcasted_iota(jnp.int32, (2, D), 1)
    keep = (row_ids < live) & (col_ids < live)
    masked_rows = jnp.where(keep, wave_ref[0].astype(F32), 0.0)
    basis_rows = basis_ref[0].astype(F32)
    for w, rows in enumerate((masked_rows, basis_rows)):
        zbuf[w, NEAR] = jnp.concatenate([rows[:, :H], rows[:, H:]], axis=0).astype(BF16)

    pl.semaphore_wait(barrier, len(greeted))

    for w in range(2):
        for d in range(NEAR, 0, -1):
            send(zbuf.at[w, NEAR], zbuf.at[w, NEAR - d], zsend_sem.at[w], zrecv_sem.at[w, 0], at_z(d))
            send(zbuf.at[w, NEAR], zbuf.at[w, NEAR + d], zsend_sem.at[w], zrecv_sem.at[w, 0], at_z(NZ - d))
        owe(zbuf.at[w, pl.ds(0, NZ - 1)], zsend_sem.at[w])

    def relay(w):
        taken(zbuf.at[w, pl.ds(0, 2 * NEAR)], zrecv_sem.at[w, 0])
        send(
            zbuf.at[w, pl.ds(5, 4)], zbuf.at[w, pl.ds(9, 4)], zsend_sem.at[w], zrecv_sem.at[w, 1], at_z(NZ - NEAR)
        )
        send(
            zbuf.at[w, pl.ds(1, 3)], zbuf.at[w, pl.ds(13, 3)], zsend_sem.at[w], zrecv_sem.at[w, 1], at_z(NEAR)
        )

    def spread(w, half):
        if half == 1:
            taken(zbuf.at[w, pl.ds(9, 7)], zrecv_sem.at[w, 1])
        pieces = zbuf[w, 8 * half : 8 * half + 8].astype(F32)
        rows = [
            jnp.concatenate([pieces[:, r, :], pieces[:, 2 + r, :]], axis=1) for r in range(2)
        ]
        block = walls[w][half].at[sec, j]
        block[...] = jnp.concatenate(rows, axis=0).astype(BF16)
        n_direct = DIRECT[w, half]
        xs, os, cs = xsend_sem.at[w, half], osend_sem.at[w, half], csend_sem.at[w, half]
        for n, step in enumerate(XY_STEPS):
            send(block, block, xs, xrecv_sem.at[w, half, n], at_plane(step))
            if n < n_direct:
                send(block, block, os, crecv_sem.at[w, half], at_plane_other(step))
        send(block, block, cs, crecv_sem.at[w, half], sibling)
        owe(blocks(NX - 1), xs)
        owe(blocks(n_direct), os)
        owe(blocks(NX - n_direct), cs)

    def blocks(count):
        return right.at[0, pl.ds(0, 16 * count)]

    def pass_on(w, half):
        for n in reversed(range(NX - 1)):
            a, b = XY_STEPS[n]
            pj, psec = place(4 - a, 4 - b)
            block = walls[w][half].at[psec, pj]
            taken(block, xrecv_sem.at[w, half, n])
            if n >= DIRECT[w, half]:
                send(block, block, csend_sem.at[w, half], crecv_sem.at[w, half], sibling)

    def passed(w, half):
        taken(walls[w][half].at[pl.ds(0, 2)], crecv_sem.at[w, half])

    def gathered_half(w, half, u):
        return walls[w][half][u].reshape(H, D)

    def gathered(w, u):
        return jnp.concatenate([gathered_half(w, half, u) for half in range(2)], axis=0)

    relay(0)
    spread(0, 0)
    relay(1)
    spread(1, 0)
    spread(0, 1)
    pass_on(0, 0)
    pass_on(1, 0)

    left_in.wait()
    for k in range(NPAIR):
        columns = nn(left[k], perm[0]).astype(BF16)
        left_near[:, k * H : (k + 1) * H] = columns[:, :H]
        left_far[:, k * H : (k + 1) * H] = columns[:, H:]

    for copy in pairs_in:
        copy.wait()

    def source(k):
        u = sec - shift_ref[k]
        inside = (u >= 0) & (u < NSEC)
        return jnp.clip(u, 0, NSEC - 1), inside

    def pair_terms(half, left_part, carried_part):
        for k in range(NPAIR):
            u, inside = source(k)
            weight = scale_ref[orb_ref[0, k]] * scale_ref[orb_ref[1, k]] * SCALE
            weight = jnp.where(inside, weight, 0.0)
            product = nt(gathered_half(0, half, u), right[k])
            carried_part[k * H : (k + 1) * H, :] = (weight * product).astype(BF16)
        return nn(left_part[...], carried_part[...])

    passed(0, 0)
    total = pair_terms(0, left_near, carried_near)
    for h in range(2):
        sig[h] = total[:, h * H : (h + 1) * H]

    pass_on(0, 1)
    spread(1, 1)
    passed(0, 1)
    total = pair_terms(1, left_far, carried_far)
    for h in range(2):
        sig[h] += total[:, h * H : (h + 1) * H]

    for t in range(NJ):
        for h in range(2):
            for r in range(2):
                rs_send[t, 2 * h + r] = sig[h, pl.ds(2 * t + r, 16, stride=16), :].astype(BF16)
    for step in J_STEPS:
        t, device = at_j(step)
        send(rs_send.at[t], rs_recv.at[j], rsend_sem, rrecv_sem, device)
    owe(rs_send.at[pl.ds(0, NJ - 1)], rsend_sem)
    rs_recv[j] = rs_send[j]

    own_wave = nn(perm[0], gathered(0, sec)).astype(BF16)
    ham_rows = nn(ham_ref[0], own_wave)
    num = jnp.sum(ham_rows * masked_rows, axis=0, keepdims=True)
    lanes = num[:, :H] + num[:, H:]
    for h in range(2):
        wide = own_wave[:, h * H : (h + 1) * H].astype(F32)
        lanes += jnp.sum(sig[h] * wide, axis=0, keepdims=True)
    place_own = sec * NJ + j
    corr_x[place_own] = lanes
    part = corr_x.at[place_own]
    for step in XY_STEPS:
        send(part, part, qsend_sem, qrecv_sem, at_plane_other(step))
        send(part, part, qsend_sem, qrecv_sem, at_plane(step))
    send(part, part, qsend_sem, qrecv_sem, sibling)
    owe(corr_x.at[pl.ds(0, 2 * NX - 1)], qsend_sem)

    def renormalize(ks):
        for k in ks:
            u, inside = source(k)
            left_basis = nn(left[k], mats[u]).astype(BF16)
            value = nn(basis_t[...], left_basis)
            renorm_ref[0, k] = jnp.where(inside, value, 0.0).astype(BF16)

    norm = jnp.zeros((D, D), F32)
    for u in range(NSEC):
        wide = gathered(0, u).astype(F32)
        norm += wide * wide
    norm = jnp.sum(jnp.sum(norm, axis=0, keepdims=True), axis=1, keepdims=True)

    taken(rs_recv.at[pl.ds(0, NJ - 1)], rrecv_sem)
    chunk = [rs_recv[0, q].astype(F32) for q in range(4)]
    for t in range(1, NJ):
        for q in range(4):
            chunk[q] += rs_recv[t, q].astype(F32)
    zs_send[...] = jnp.stack(chunk, axis=1).astype(BF16)
    for i in Z_STEPS:
        send(zs_send.at[(z + i) % NZ], zs_recv.at[z], ssend_sem, srecv_sem, at_z(i))
    owe(zs_send.at[pl.ds(0, NZ - 1)], ssend_sem)

    taken(corr_x.at[pl.ds(0, 2 * NX - 1)], qrecv_sem)
    corr_zown[...] = jnp.sum(corr_x[...], axis=0)
    for i in Z_STEPS:
        send(corr_zown, corr_z.at[z], tsend_sem, trecv_sem, at_z(i))
    owe(corr_z.at[pl.ds(0, NZ - 1)], tsend_sem)
    zs_recv[z] = zs_send[z]
    corr_z[z] = corr_zown[...]

    pass_on(1, 1)
    passed(1, 0)
    passed(1, 1)
    for u in range(NSEC):
        mats[u] = nn(perm[0], gathered(1, u)).astype(BF16)
    basis_t[...] = nt(perm[1], mats[sec]).astype(BF16)

    renormalize(range(NPAIR))

    taken(zs_recv.at[pl.ds(0, NZ - 1)], srecv_sem)
    summed = jnp.sum(zs_recv[...].astype(F32), axis=0)
    taken(corr_z.at[pl.ds(0, NZ - 1)], trecv_sem)
    energy = jnp.sum(jnp.sum(corr_z[...], axis=0), axis=1, keepdims=True) / norm
    for h in range(2):
        rows = summed[2 * h : 2 * h + 2, :] + ham_rows[:, h * H : (h + 1) * H]
        resid_ref[0, :, h * H : (h + 1) * H] = rows - energy * masked_rows[:, h * H : (h + 1) * H]

    for wait in sent:
        wait()


def on_device(
    wave,
    sector_live,
    left_ops,
    right_ops,
    pair_shift,
    pair_orbitals,
    orbital_scale,
    block_ham,
    site_basis,
):
    vmem = pl.BlockSpec(memory_space=pltpu.VMEM)
    hbm = pl.BlockSpec(memory_space=pltpu.HBM)
    dma = pltpu.SemaphoreType.DMA

    def in_hbm(value):
        return pltpu.with_memory_space_constraint(value, pltpu.HBM)

    return pl.pallas_call(
        kernel,
        out_shape=(
            jax.ShapeDtypeStruct((1, 2, D), F32),
            jax.ShapeDtypeStruct((1, NPAIR, D, D), BF16),
        ),
        in_specs=[hbm] * 9,
        out_specs=(vmem, vmem),
        scratch_shapes=[
            pltpu.SMEM((1, 1), jnp.int32),
            pltpu.SMEM((NPAIR,), jnp.int32),
            pltpu.SMEM((2, NPAIR), jnp.int32),
            pltpu.SMEM((NORB,), F32),
            pltpu.VMEM((1, 2, D), BF16),
            pltpu.VMEM((1, 2, D), BF16),
            pltpu.VMEM((1, 2, D), BF16),
            pltpu.VMEM((NPAIR, D, D), BF16),
            pltpu.VMEM((NPAIR, D, D), BF16),
            pltpu.VMEM((D, NPAIR * H), BF16),
            pltpu.VMEM((D, NPAIR * H), BF16),
            pltpu.VMEM((NPAIR * H, D), BF16),
            pltpu.VMEM((NPAIR * H, D), BF16),
            pltpu.VMEM((2, NZ, 4, H), BF16),
            pltpu.VMEM((NSEC, NJ, 16, D), BF16),
            pltpu.VMEM((NSEC, NJ, 16, D), BF16),
            pltpu.VMEM((NSEC, NJ, 16, D), BF16),
            pltpu.VMEM((NSEC, NJ, 16, D), BF16),
            pltpu.VMEM((NSEC, D, D), BF16),
            pltpu.VMEM((2, D, D), BF16),
            pltpu.VMEM((D, D), BF16),
            pltpu.VMEM((2, D, H), F32),
            pltpu.VMEM((NJ, 4, NZ, H), BF16),
            pltpu.VMEM((NJ, 4, NZ, H), BF16),
            pltpu.VMEM((2 * NX, 1, H), F32),
            pltpu.VMEM((1, H), F32),
            pltpu.VMEM((NZ, 1, H), F32),
            pltpu.VMEM((NZ, 4, H), BF16),
            pltpu.VMEM((NZ, 4, H), BF16),
            dma((7,)),
            dma((2,)),
            dma((2,)),
            dma((2, 2)),
            dma((2, 2)),
            dma((2, 2)),
            dma((2, 2, NX)),
            dma((2, 2)),
            dma((2, 2)),
            dma,
            dma,
            dma,
            dma,
            dma,
            dma,
            dma,
            dma,
        ],
        compiler_params=pltpu.CompilerParams(
            collective_id=0, has_side_effects=True, vmem_limit_bytes=48 * 1024 * 1024
        ),
        cost_estimate=pl.CostEstimate(flops=1900000000, bytes_accessed=4800000, transcendentals=0),
    )(
        sector_live.reshape(1, 1),
        in_hbm(pair_shift),
        in_hbm(pair_orbitals.T),
        in_hbm(orbital_scale),
        in_hbm(wave),
        in_hbm(block_ham),
        in_hbm(site_basis),
        in_hbm(left_ops),
        in_hbm(right_ops),
    )


def solution(mesh):
    placed = (
        P("sec", "ops", None),
        P("sec"),
        P("sec", "ops", None, None),
        P("sec", "ops", None, None),
        P("ops"),
        P("ops", None),
        P(),
        P("sec", "ops", None),
        P("sec", "ops", None),
    )
    return jax.shard_map(
        on_device,
        mesh=mesh,
        in_specs=placed,
        out_specs=(P("sec", "ops", None), P("sec", "ops", None, None)),
        check_vma=False,
    )
```

```python
import functools
import math

import jax
import jax.numpy as jnp
from jax import lax
from jax.experimental import pallas as pl
from jax.experimental.pallas import tpu as pltpu
from jax.sharding import PartitionSpec as P

MESH = pl.DeviceIdType.MESH
F32 = jnp.float32
BF16 = jnp.bfloat16
NZ = 16
NJ = 8
NX = 16
NSEC = 4
NPAIR = 12
NORB = 120
D = 256
H = 128
SCALE = 1.0 / math.sqrt(256 * 1536)

NEAR = 4
DIRECT = {(0, 0): 1, (0, 1): 1, (1, 0): 1, (1, 1): 1}

Z_STEPS = sorted(range(1, NZ), key=lambda i: -min(i, NZ - i))
XY_STEPS = sorted(
    [(a, b) for a in range(4) for b in range(4) if a or b],
    key=lambda s: -(min(s[0], 4 - s[0]) + min(s[1], 4 - s[1])),
)
J_STEPS = sorted(
    [(a, b) for a in range(2) for b in range(4) if a or b],
    key=lambda s: -(2 * s[0] + min(s[1], 4 - s[1])),
)


def nt(a, b):
    return lax.dot_general(a, b, (((1,), (1,)), ((), ())), preferred_element_type=F32)


def nn(a, b):
    return jnp.dot(a, b, preferred_element_type=F32)


def kernel(
    live_hbm,
    shift_hbm,
    orb_hbm,
    scale_hbm,
    wave_hbm,
    ham_hbm,
    basis_hbm,
    left_hbm,
    right_hbm,
    resid_ref,
    renorm_ref,
    live_ref,
    shift_ref,
    orb_ref,
    scale_ref,
    wave_ref,
    ham_ref,
    basis_ref,
    left,
    right,
    left_near,
    left_far,
    carried_near,
    carried_far,
    zbuf,
    wall_wave_near,
    wall_wave_far,
    wall_basis_near,
    wall_basis_far,
    mats,
    perm,
    basis_t,
    sig,
    rs_send,
    rs_recv,
    corr_x,
    corr_zown,
    corr_z,
    zs_send,
    zs_recv,
    small_sem,
    load_sem,
    zsend_sem,
    zrecv_sem,
    xsend_sem,
    osend_sem,
    xrecv_sem,
    csend_sem,
    crecv_sem,
    rsend_sem,
    rrecv_sem,
    qsend_sem,
    qrecv_sem,
    ssend_sem,
    srecv_sem,
    tsend_sem,
    trecv_sem,
):
    walls = ((wall_wave_near, wall_wave_far), (wall_basis_near, wall_basis_far))
    ops = lax.axis_index("ops")
    sec = lax.axis_index("sec")
    z = ops // NJ
    j = ops % NJ
    x_hi = j // 4
    y = j % 4
    x_lo = sec // 2
    core = sec % 2
    x = x_hi * 2 + x_lo

    def at_z(i):
        return {"ops": ((z + i) % NZ) * NJ + j, "sec": sec}

    def place(a, b):
        px, py = (x + a) % 4, (y + b) % 4
        return (px // 2) * 4 + py, (px % 2) * 2 + core

    def at_plane(step):
        pj, psec = place(*step)
        return {"ops": z * NJ + pj, "sec": psec}

    def at_plane_other(step):
        pj, psec = place(*step)
        return {"ops": z * NJ + pj, "sec": psec + 1 - 2 * core}

    def at_j(step):
        t = ((x_hi + step[0]) % 2) * 4 + (y + step[1]) % 4
        return t, {"ops": z * NJ + t, "sec": sec}

    sibling = {"ops": ops, "sec": x_lo * 2 + (1 - core)}

    def send(src, dst, send_sem, recv_sem, device):
        pltpu.make_async_remote_copy(
            src_ref=src,
            dst_ref=dst,
            send_sem=send_sem,
            recv_sem=recv_sem,
            device_id=device,
            device_id_type=MESH,
        ).start()

    def taken(ref, sem):
        pltpu.make_async_copy(ref, ref, sem).wait()

    sent = []

    def owe(ref, sem):
        sent.append(lambda: taken(ref, sem))

    barrier = pltpu.get_barrier_semaphore()
    greeted = [at_z(i) for d in range(NEAR, 0, -1) for i in (d, NZ - d)]
    greeted += [at_plane(step) for step in XY_STEPS] + [sibling]
    greeted += [at_plane_other(step) for step in XY_STEPS[: max(DIRECT.values())]]
    for device in greeted:
        pl.semaphore_signal(barrier, inc=1, device_id=device, device_id_type=MESH)

    rows_in = (
        pltpu.make_async_copy(live_hbm, live_ref, small_sem.at[0]),
        pltpu.make_async_copy(wave_hbm, wave_ref, small_sem.at[1]),
        pltpu.make_async_copy(basis_hbm, basis_ref, small_sem.at[2]),
    )
    pairs_in = (
        pltpu.make_async_copy(ham_hbm, ham_ref, small_sem.at[3]),
        pltpu.make_async_copy(shift_hbm, shift_ref, small_sem.at[4]),
        pltpu.make_async_copy(orb_hbm, orb_ref, small_sem.at[5]),
        pltpu.make_async_copy(scale_hbm, scale_ref, small_sem.at[6]),
        pltpu.make_async_copy(right_hbm.at[0], right, load_sem.at[0]),
    )
    left_in = pltpu.make_async_copy(left_hbm.at[0], left, load_sem.at[1])
    for copy in rows_in + pairs_in + (left_in,):
        copy.start()

    m_ids = lax.broadcasted_iota(jnp.int32, (D, D), 0)
    g_ids = lax.broadcasted_iota(jnp.int32, (D, D), 1)
    s_ids = lax.rem(m_ids // 16 + (NZ + NEAR) - z, NZ)
    wanted = (s_ids // 8) * 128 + ((m_ids % 16) // 2) * 16 + (m_ids % 2) * 8 + s_ids % 8
    perm[0] = jnp.where(wanted == g_ids, 1.0, 0.0).astype(BF16)
    perm[1] = jnp.where(m_ids == g_ids, 1.0, 0.0).astype(BF16)

    for copy in rows_in:
        copy.wait()
    live = live_ref[0, 0]
    row_ids = ops * 2 + lax.broadcasted_iota(jnp.int32, (2, D), 0)
    col_ids = lax.broadcasted_iota(jnp.int32, (2, D), 1)
    keep = (row_ids < live) & (col_ids < live)
    masked_rows = jnp.where(keep, wave_ref[0].astype(F32), 0.0)
    basis_rows = basis_ref[0].astype(F32)
    for w, rows in enumerate((masked_rows, basis_rows)):
        zbuf[w, NEAR] = jnp.concatenate([rows[:, :H], rows[:, H:]], axis=0).astype(BF16)

    pl.semaphore_wait(barrier, len(greeted))

    for w in range(2):
        for d in range(NEAR, 0, -1):
            send(zbuf.at[w, NEAR], zbuf.at[w, NEAR - d], zsend_sem.at[w], zrecv_sem.at[w, 0], at_z(d))
            send(zbuf.at[w, NEAR], zbuf.at[w, NEAR + d], zsend_sem.at[w], zrecv_sem.at[w, 0], at_z(NZ - d))
        owe(zbuf.at[w, pl.ds(0, NZ - 1)], zsend_sem.at[w])

    def relay(w):
        taken(zbuf.at[w, pl.ds(0, 2 * NEAR)], zrecv_sem.at[w, 0])
        send(
            zbuf.at[w, pl.ds(5, 4)], zbuf.at[w, pl.ds(9, 4)], zsend_sem.at[w], zrecv_sem.at[w, 1], at_z(NZ - NEAR)
        )
        send(
            zbuf.at[w, pl.ds(1, 3)], zbuf.at[w, pl.ds(13, 3)], zsend_sem.at[w], zrecv_sem.at[w, 1], at_z(NEAR)
        )

    def spread(w, half):
        if half == 1:
            taken(zbuf.at[w, pl.ds(9, 7)], zrecv_sem.at[w, 1])
        pieces = zbuf[w, 8 * half : 8 * half + 8].astype(F32)
        rows = [
            jnp.concatenate([pieces[:, r, :], pieces[:, 2 + r, :]], axis=1) for r in range(2)
        ]
        block = walls[w][half].at[sec, j]
        block[...] = jnp.concatenate(rows, axis=0).astype(BF16)
        n_direct = DIRECT[w, half]
        xs, os, cs = xsend_sem.at[w, half], osend_sem.at[w, half], csend_sem.at[w, half]
        for n, step in enumerate(XY_STEPS):
            send(block, block, xs, xrecv_sem.at[w, half, n], at_plane(step))
            if n < n_direct:
                send(block, block, os, crecv_sem.at[w, half], at_plane_other(step))
        send(block, block, cs, crecv_sem.at[w, half], sibling)
        owe(blocks(NX - 1), xs)
        owe(blocks(n_direct), os)
        owe(blocks(NX - n_direct), cs)

    def blocks(count):
        return right.at[0, pl.ds(0, 16 * count)]

    def pass_on(w, half):
        for n in reversed(range(NX - 1)):
            a, b = XY_STEPS[n]
            pj, psec = place(4 - a, 4 - b)
            block = walls[w][half].at[psec, pj]
            taken(block, xrecv_sem.at[w, half, n])
            if n >= DIRECT[w, half]:
                send(block, block, csend_sem.at[w, half], crecv_sem.at[w, half], sibling)

    def passed(w, half):
        taken(walls[w][half].at[pl.ds(0, 2)], crecv_sem.at[w, half])

    def gathered_half(w, half, u):
        return walls[w][half][u].reshape(H, D)

    def gathered(w, u):
        return jnp.concatenate([gathered_half(w, half, u) for half in range(2)], axis=0)

    relay(0)
    spread(0, 0)
    relay(1)
    spread(1, 0)
    spread(0, 1)
    pass_on(0, 0)
    pass_on(1, 0)

    left_in.wait()
    for k in range(NPAIR):
        columns = nn(left[k], perm[0]).astype(BF16)
        left_near[:, k * H : (k + 1) * H] = columns[:, :H]
        left_far[:, k * H : (k + 1) * H] = columns[:, H:]

    for copy in pairs_in:
        copy.wait()

    def source(k):
        u = sec - shift_ref[k]
        inside = (u >= 0) & (u < NSEC)
        return jnp.clip(u, 0, NSEC - 1), inside

    def pair_terms(half, left_part, carried_part):
        for k in range(NPAIR):
            u, inside = source(k)
            weight = scale_ref[orb_ref[0, k]] * scale_ref[orb_ref[1, k]] * SCALE
            weight = jnp.where(inside, weight, 0.0)
            product = nt(gathered_half(0, half, u), right[k])
            carried_part[k * H : (k + 1) * H, :] = (weight * product).astype(BF16)
        return nn(left_part[...], carried_part[...])

    passed(0, 0)
    total = pair_terms(0, left_near, carried_near)
    for h in range(2):
        sig[h] = total[:, h * H : (h + 1) * H]

    pass_on(0, 1)
    spread(1, 1)
    passed(0, 1)
    total = pair_terms(1, left_far, carried_far)
    for h in range(2):
        sig[h] += total[:, h * H : (h + 1) * H]

    for t in range(NJ):
        for h in range(2):
            for r in range(2):
                rs_send[t, 2 * h + r] = sig[h, pl.ds(2 * t + r, 16, stride=16), :].astype(BF16)
    for step in J_STEPS:
        t, device = at_j(step)
        send(rs_send.at[t], rs_recv.at[j], rsend_sem, rrecv_sem, device)
    owe(rs_send.at[pl.ds(0, NJ - 1)], rsend_sem)
    rs_recv[j] = rs_send[j]

    own_wave = nn(perm[0], gathered(0, sec)).astype(BF16)
    ham_rows = nn(ham_ref[0], own_wave)
    num = jnp.sum(ham_rows * masked_rows, axis=0, keepdims=True)
    lanes = num[:, :H] + num[:, H:]
    for h in range(2):
        wide = own_wave[:, h * H : (h + 1) * H].astype(F32)
        lanes += jnp.sum(sig[h] * wide, axis=0, keepdims=True)
    place_own = sec * NJ + j
    corr_x[place_own] = lanes
    part = corr_x.at[place_own]
    for step in XY_STEPS:
        send(part, part, qsend_sem, qrecv_sem, at_plane_other(step))
        send(part, part, qsend_sem, qrecv_sem, at_plane(step))
    send(part, part, qsend_sem, qrecv_sem, sibling)
    owe(corr_x.at[pl.ds(0, 2 * NX - 1)], qsend_sem)

    def renormalize(ks):
        for k in ks:
            u, inside = source(k)
            left_basis = nn(left[k], mats[u]).astype(BF16)
            value = nn(basis_t[...], left_basis)
            renorm_ref[0, k] = jnp.where(inside, value, 0.0).astype(BF16)

    norm = jnp.zeros((D, D), F32)
    for u in range(NSEC):
        wide = gathered(0, u).astype(F32)
        norm += wide * wide
    norm = jnp.sum(jnp.sum(norm, axis=0, keepdims=True), axis=1, keepdims=True)

    taken(rs_recv.at[pl.ds(0, NJ - 1)], rrecv_sem)
    chunk = [rs_recv[0, q].astype(F32) for q in range(4)]
    for t in range(1, NJ):
        for q in range(4):
            chunk[q] += rs_recv[t, q].astype(F32)
    for q in range(4):
        zs_send[:, q, :] = chunk[q]
    for i in Z_STEPS:
        send(zs_send.at[(z + i) % NZ], zs_recv.at[z], ssend_sem, srecv_sem, at_z(i))
    owe(zs_send.at[pl.ds(0, NZ - 1)], ssend_sem)

    taken(corr_x.at[pl.ds(0, 2 * NX - 1)], qrecv_sem)
    corr_zown[...] = jnp.sum(corr_x[...], axis=0)

    @pl.when(core == 1)
    def _():
        for i in Z_STEPS:
            send(corr_zown, corr_z.at[z], tsend_sem, trecv_sem, {"ops": at_z(i)["ops"], "sec": sec - 1})
            send(corr_zown, corr_z.at[z], tsend_sem, trecv_sem, at_z(i))
        send(corr_zown, corr_z.at[z], tsend_sem, trecv_sem, {"ops": ops, "sec": sec - 1})
        corr_z[z] = corr_zown[...]

    zs_recv[z] = zs_send[z]

    pass_on(1, 1)
    passed(1, 0)
    passed(1, 1)
    for u in range(NSEC):
        mats[u] = nn(perm[0], gathered(1, u)).astype(BF16)
    basis_t[...] = nt(perm[1], mats[sec]).astype(BF16)

    renormalize(range(NPAIR))

    taken(zs_recv.at[pl.ds(0, NZ - 1)], srecv_sem)
    summed = jnp.sum(zs_recv[...], axis=0)

    @pl.when(core == 0)
    def _():
        taken(corr_z, trecv_sem)

    @pl.when(core == 1)
    def _():
        taken(corr_z.at[pl.ds(0, NZ - 1)], trecv_sem)

    energy = jnp.sum(jnp.sum(corr_z[...], axis=0), axis=1, keepdims=True) / norm
    for h in range(2):
        rows = summed[2 * h : 2 * h + 2, :] + ham_rows[:, h * H : (h + 1) * H]
        resid_ref[0, :, h * H : (h + 1) * H] = rows - energy * masked_rows[:, h * H : (h + 1) * H]

    for wait in sent:
        wait()

    @pl.when(core == 1)
    def _():
        taken(corr_x.at[pl.ds(0, 2 * NX - 1)], tsend_sem)


def on_device(
    wave,
    sector_live,
    left_ops,
    right_ops,
    pair_shift,
    pair_orbitals,
    orbital_scale,
    block_ham,
    site_basis,
):
    vmem = pl.BlockSpec(memory_space=pltpu.VMEM)
    hbm = pl.BlockSpec(memory_space=pltpu.HBM)
    dma = pltpu.SemaphoreType.DMA

    def in_hbm(value):
        return pltpu.with_memory_space_constraint(value, pltpu.HBM)

    return pl.pallas_call(
        kernel,
        out_shape=(
            jax.ShapeDtypeStruct((1, 2, D), F32),
            jax.ShapeDtypeStruct((1, NPAIR, D, D), BF16),
        ),
        in_specs=[hbm] * 9,
        out_specs=(vmem, vmem),
        scratch_shapes=[
            pltpu.SMEM((1, 1), jnp.int32),
            pltpu.SMEM((NPAIR,), jnp.int32),
            pltpu.SMEM((2, NPAIR), jnp.int32),
            pltpu.SMEM((NORB,), F32),
            pltpu.VMEM((1, 2, D), BF16),
            pltpu.VMEM((1, 2, D), BF16),
            pltpu.VMEM((1, 2, D), BF16),
            pltpu.VMEM((NPAIR, D, D), BF16),
            pltpu.VMEM((NPAIR, D, D), BF16),
            pltpu.VMEM((D, NPAIR * H), BF16),
            pltpu.VMEM((D, NPAIR * H), BF16),
            pltpu.VMEM((NPAIR * H, D), BF16),
            pltpu.VMEM((NPAIR * H, D), BF16),
            pltpu.VMEM((2, NZ, 4, H), BF16),
            pltpu.VMEM((NSEC, NJ, 16, D), BF16),
            pltpu.VMEM((NSEC, NJ, 16, D), BF16),
            pltpu.VMEM((NSEC, NJ, 16, D), BF16),
            pltpu.VMEM((NSEC, NJ, 16, D), BF16),
            pltpu.VMEM((NSEC, D, D), BF16),
            pltpu.VMEM((2, D, D), BF16),
            pltpu.VMEM((D, D), BF16),
            pltpu.VMEM((2, D, H), F32),
            pltpu.VMEM((NJ, 4, NZ, H), BF16),
            pltpu.VMEM((NJ, 4, NZ, H), BF16),
            pltpu.VMEM((2 * NX, 1, H), F32),
            pltpu.VMEM((1, H), F32),
            pltpu.VMEM((NZ, 1, H), F32),
            pltpu.VMEM((NZ, 4, H), F32),
            pltpu.VMEM((NZ, 4, H), F32),
            dma((7,)),
            dma((2,)),
            dma((2,)),
            dma((2, 2)),
            dma((2, 2)),
            dma((2, 2)),
            dma((2, 2, NX)),
            dma((2, 2)),
            dma((2, 2)),
            dma,
            dma,
            dma,
            dma,
            dma,
            dma,
            dma,
            dma,
        ],
        compiler_params=pltpu.CompilerParams(
            collective_id=0, has_side_effects=True, vmem_limit_bytes=48 * 1024 * 1024
        ),
        cost_estimate=pl.CostEstimate(flops=1900000000, bytes_accessed=4800000, transcendentals=0),
    )(
        sector_live.reshape(1, 1),
        in_hbm(pair_shift),
        in_hbm(pair_orbitals.T),
        in_hbm(orbital_scale),
        in_hbm(wave),
        in_hbm(block_ham),
        in_hbm(site_basis),
        in_hbm(left_ops),
        in_hbm(right_ops),
    )


def solution(mesh):
    placed = (
        P("sec", "ops", None),
        P("sec"),
        P("sec", "ops", None, None),
        P("sec", "ops", None, None),
        P("ops"),
        P("ops", None),
        P(),
        P("sec", "ops", None),
        P("sec", "ops", None),
    )
    return jax.shard_map(
        on_device,
        mesh=mesh,
        in_specs=placed,
        out_specs=(P("sec", "ops", None), P("sec", "ops", None, None)),
        check_vma=False,
    )
```
